128 devices in a mesh: qrow: 32 (over x, y_lo, z), kcol: 4 (over y_hi, core).
Axes of the slice: x: 4, y: 4 (y_hi: 2, y_lo: 2; y = y_hi * 2 + y_lo), z: 4, core: 2. Of those that a mesh axis runs over, the one named last changes fastest.
Arguments:
- queries: bfloat16 [16384, 1024], P(('qrow', 'kcol')), may hold values from -6 to 6
- key_states: bfloat16 [16384, 128], P(('qrow', 'kcol')), may hold values from -6 to 6
- value_states: bfloat16 [16384, 128], P(('qrow', 'kcol')), may hold values from -6 to 6
- out_grad: bfloat16 [16384, 1024], P(('qrow', 'kcol')), may hold values from -6 to 6
- forward_out: bfloat16 [16384, 1024], P(('qrow', 'kcol')), may hold values from -1.1953125 to 1.1953125
- stretch_order: int32 [128], replicated, may hold values from 0 to 127, each once
Outputs:
- d_query: bfloat16 [16384, 1024], P(('qrow', 'kcol'))
- d_key: bfloat16 [16384, 128], P(('qrow', 'kcol'))
- d_value: bfloat16 [16384, 128], P(('qrow', 'kcol'))
The draws below stay inside these ranges and needn't reach their ends.
Inputs may be any that keep to these rules, and one draw needn't show every extreme that they name: `stretch_order`: every stretch number appears once.
All inputs are finite; a program needn't handle non-finite values.
Results may differ from the reference program's by a relative error of at most 0.018.
Values may be sent and summed in bfloat16 or wider, within the bound.
No kernel may reach another device: no remote copies, remote signals or barrier semaphores. Data moves between devices by JAX's collectives and lax.ppermute only.
A program may use at most 128 MiB of HBM per device.

```python
import jax
import jax.numpy as jnp
from jax import lax

H = 8
HD = 128
CH = 128
STRETCHES = 128
SEQ = 16384


def draw_queries(key, part):
    key = jax.random.fold_in(key, 1)
    values = jax.random.truncated_normal(key, -4.0, 4.0, (STRETCHES, CH, H, HD), jnp.float32)
    return values.reshape(STRETCHES * CH, H * HD).astype(jnp.bfloat16)


def draw_key_states(key, part):
    key = jax.random.fold_in(key, 2)
    values = jax.random.truncated_normal(key, -4.0, 4.0, (STRETCHES, CH, HD), jnp.float32)
    return values.reshape(STRETCHES * CH, HD).astype(jnp.bfloat16)


def level_of(own_key, extent, split, low, largest):
    gain = 1.0
    for position, parts in split:
        steps = jax.random.uniform(jax.random.fold_in(jax.random.fold_in(own_key, 6), position), (parts,), jnp.float32, low / len(split), largest / len(split))
        gain = gain * jnp.repeat(jnp.exp(steps), extent[position] // parts).reshape((-1,) + (1,) * (len(extent) - 1 - position))
    return gain


def gaussian(key, extent, spread, limit, shards=(), held_as=jnp.bfloat16):
    drawn = spread * jax.random.normal(key, extent, jnp.float32)
    if shards:
        drawn = drawn * level_of(key, extent, shards, -0.22, 0.18)
    return jnp.clip(drawn, -limit, limit).astype(held_as)


def setup_inputs(seed: int = 0) -> dict:
    seeds = jax.random.split(jax.random.key(seed), 7)
    queries = draw_queries(jax.random.fold_in(seeds[6], 71), 0)
    key_states = draw_key_states(jax.random.fold_in(seeds[6], 71), 0)
    value_states = gaussian(seeds[2], (SEQ, HD), 1.0, 6.0, ((0, 128),))
    out_grad = gaussian(seeds[3], (SEQ, H * HD), 1.0, 6.0, ((0, 128),))
    forward_out = gaussian(seeds[4], (SEQ, H * HD), 0.2, 1.1953125, ((0, 128),))
    stretch_order = jax.random.permutation(seeds[5], STRETCHES).astype(jnp.int32)
    return dict(queries=queries, key_states=key_states, value_states=value_states, out_grad=out_grad, forward_out=forward_out, stretch_order=stretch_order)


NEGATIVE = -1.0e30


def contract(left, right, left_dim, right_dim):
    return lax.dot_general(left, right, (((left_dim,), (right_dim,)), ((), ())), preferred_element_type=jnp.float32)


def reference(queries, key_states, value_states, out_grad, forward_out, stretch_order):
    total = queries.shape[0]
    heads = queries.shape[1] // HD
    scale = float(HD) ** -0.5
    places = (stretch_order[:, None] * CH + jnp.arange(CH, dtype=jnp.int32)[None, :]).reshape(-1).astype(jnp.int32)
    products = out_grad.astype(jnp.float32) * forward_out.astype(jnp.float32)
    delta = jnp.sum(products.reshape(total, heads, HD), axis=2).astype(jnp.bfloat16)
    block = min(512, total)
    count = total // block
    height = block * heads
    query_blocks = queries.reshape(count, height, HD)
    grad_blocks = out_grad.reshape(count, height, HD)
    delta_blocks = delta.reshape(count, height)
    place_blocks = jnp.repeat(places, heads).reshape(count, height)

    def totals_step(carry, pieces):
        query_rows, query_places = pieces
        scores = contract(query_rows, key_states, 1, 1) * scale
        allowed = places[None, :] <= query_places[:, None]
        peak = jnp.max(jnp.where(allowed, scores, NEGATIVE), axis=1)
        summed = jnp.sum(jnp.where(allowed, jnp.exp(scores - peak[:, None]), 0.0), axis=1)
        return carry, peak + jnp.log(summed)

    _, log_blocks = lax.scan(totals_step, jnp.zeros((), jnp.float32), (query_blocks, place_blocks))

    def grad_step(carry, pieces):
        key_total, value_total = carry
        query_rows, grad_rows, delta_rows, log_rows, query_places = pieces
        scores = contract(query_rows, key_states, 1, 1) * scale
        allowed = places[None, :] <= query_places[:, None]
        probs = jnp.where(allowed, jnp.exp(scores - log_rows[:, None]), 0.0)
        probs_low = probs.astype(jnp.bfloat16)
        value_total = value_total + contract(probs_low, grad_rows, 0, 0)
        dprobs = contract(grad_rows, value_states, 1, 1)
        dscores = (probs * (dprobs - delta_rows.astype(jnp.float32)[:, None])).astype(jnp.bfloat16)
        query_part = jnp.dot(dscores, key_states, preferred_element_type=jnp.float32)
        key_total = key_total + contract(dscores, query_rows, 0, 0)
        return (key_total, value_total), query_part

    zeros = jnp.zeros((total, HD), jnp.float32)
    (key_total, value_total), query_parts = lax.scan(grad_step, (zeros, zeros), (query_blocks, grad_blocks, delta_blocks, log_blocks, place_blocks))
    d_query = (query_parts.reshape(total, heads * HD) * scale).astype(jnp.bfloat16)
    d_key = (key_total * scale).astype(jnp.bfloat16)
    d_value = value_total.astype(jnp.bfloat16)
    return (d_query, d_key, d_value)
```

```python
import jax
import jax.numpy as jnp
from jax import lax
from jax.experimental import pallas as pl
from jax.experimental.pallas import tpu as pltpu
from jax.sharding import PartitionSpec as P

ALL = ("qrow", "kcol")
DEVICES = 128
HEADS = 8
WIDTH = 128
STRETCH = 128
PLACES = 128
KEY_GROUPS = 4
ROW_GROUPS = 32
QUERY_TOKENS = STRETCH // ROW_GROUPS
KEY_TOKENS = STRETCH // KEY_GROUPS
HALF = KEY_TOKENS // 2
ROWS = QUERY_TOKENS * HEADS
ALL_ROWS = PLACES * ROWS
ALL_KEYS = PLACES * KEY_TOKENS
TILE = 512
TILES = ALL_ROWS // TILE
SPAN = TILE // ROWS
NEGATIVE = -1e30
SCALE = float(WIDTH) ** (-0.5)
TO_LOG2 = SCALE * 1.4426950408889634
VMEM = 56 * 1024 * 1024


def contract(left, right, left_dim, right_dim):
    return lax.dot_general(
        left, right, (((left_dim,), (right_dim,)), ((), ())), preferred_element_type=jnp.float32
    )


def tile_at(index):
    return pl.ds(pl.multiple_of(index * TILE, TILE), TILE)


def allowed_on_diagonal(key_group, row_group):
    row = lax.broadcasted_iota(jnp.int32, (TILE, TILE), 0)
    column = lax.broadcasted_iota(jnp.int32, (TILE, TILE), 1)
    row_place = (row // ROWS) * STRETCH + row_group * QUERY_TOKENS + (row % ROWS) // HEADS
    key_place = (column // KEY_TOKENS) * STRETCH + key_group * KEY_TOKENS + column % KEY_TOKENS
    return key_place <= row_place


def stats_kernel(table, moved, other_half, stats, query, key, peak, total):
    key_group, row_group, core = table[PLACES], table[PLACES + 1], table[PLACES + 2]

    def sort(place, carry):
        source = table[place]
        query[pl.ds(pl.multiple_of(place * ROWS, ROWS), ROWS)] = moved[source, 0:ROWS]
        first = pl.multiple_of(place * KEY_TOKENS + core * HALF, HALF)
        second = pl.multiple_of(place * KEY_TOKENS + (1 - core) * HALF, HALF)
        key[pl.ds(first, HALF)] = moved[source, 2 * ROWS : 2 * ROWS + HALF]
        key[pl.ds(second, HALF)] = other_half[source, 0:HALF]
        return carry

    lax.fori_loop(0, PLACES, sort, 0)
    lane = lax.broadcasted_iota(jnp.int32, (TILE, WIDTH), 1)

    def per_row_tile(i, packed):
        rows = query[tile_at(i)]
        peak[...] = jnp.full_like(peak, NEGATIVE)
        total[...] = jnp.zeros_like(total)

        def absorb(scores):
            parts = [scores[:, k * WIDTH : (k + 1) * WIDTH] for k in range(TILE // WIDTH)]
            highest = peak[...]
            old = highest
            for part in parts:
                highest = jnp.maximum(highest, part)
            summed = total[...] * jnp.exp2((old - highest) * TO_LOG2)
            for part in parts:
                summed = summed + jnp.exp2((part - highest) * TO_LOG2)
            peak[...] = highest
            total[...] = summed

        def full_tile(j, carry):
            absorb(contract(rows, key[tile_at(j)], 1, 1))
            return carry

        lax.fori_loop(0, i, full_tile, 0)
        scores = contract(rows, key[tile_at(i)], 1, 1)
        absorb(jnp.where(allowed_on_diagonal(key_group, row_group), scores, NEGATIVE))
        row_peak = jnp.max(peak[...], axis=1, keepdims=True)
        row_total = jnp.sum(
            total[...] * jnp.exp2((peak[...] - row_peak) * TO_LOG2), axis=1, keepdims=True
        )
        packed = jnp.where(lane == i, row_peak, packed)
        return jnp.where(lane == i + TILES, row_total, packed)

    packed = lax.fori_loop(0, TILES, per_row_tile, jnp.zeros((TILE, WIDTH), jnp.float32))
    stats[...] = packed.T[0 : 2 * TILES]


def gradient_kernel(
    table,
    moved,
    other_half,
    delta,
    stats_0,
    stats_1,
    stats_2,
    stats_3,
    query_grad,
    own_grad,
    other_grad,
    query,
    grad,
    key,
    value,
    query_turned,
    grad_turned,
    logs,
    query_total,
    key_total,
    value_total,
    key_sorted,
    value_sorted,
):
    key_group, row_group, core = table[PLACES], table[PLACES + 1], table[PLACES + 2]
    lane = lax.broadcasted_iota(jnp.int32, (TILE, WIDTH), 1)
    all_stats = [ref[...] for ref in (stats_0, stats_1, stats_2, stats_3)]
    peaks = [part[0:TILES] for part in all_stats]
    highest = jnp.maximum(jnp.maximum(peaks[0], peaks[1]), jnp.maximum(peaks[2], peaks[3]))
    summed = jnp.zeros_like(highest)
    for part in all_stats:
        summed = summed + part[TILES:] * jnp.exp2((part[0:TILES] - highest) * TO_LOG2)
    log_totals = highest + jnp.log2(summed) * (1.0 / TO_LOG2)
    high = log_totals.astype(jnp.bfloat16).astype(jnp.float32)
    middle = (log_totals - high).astype(jnp.bfloat16).astype(jnp.float32)
    low = (log_totals - high - middle).astype(jnp.bfloat16).astype(jnp.float32)
    padding = jnp.zeros((WIDTH - 3 * TILES, TILE), jnp.float32)
    logs[...] = jnp.concatenate([high, middle, low, padding], axis=0).T

    extra_lane = lax.broadcasted_iota(jnp.int32, (ALL_KEYS, WIDTH), 1)
    key[:, WIDTH:] = jnp.where(extra_lane < 3 * TILES, -1.0, 0.0).astype(jnp.bfloat16)
    value[:, WIDTH:] = jnp.where(extra_lane < ROWS, -1.0, 0.0).astype(jnp.bfloat16)
    row_sub = lax.broadcasted_iota(jnp.int32, (ROWS, WIDTH), 0)
    row_lane = lax.broadcasted_iota(jnp.int32, (ROWS, WIDTH), 1)

    def sort(place, carry):
        source = table[place]
        spot = pl.ds(pl.multiple_of(place * ROWS, ROWS), ROWS)
        query[spot, 0:WIDTH] = moved[source, 0:ROWS]
        grad[spot, 0:WIDTH] = moved[source, ROWS : 2 * ROWS]
        grad[spot, WIDTH:] = jnp.where(
            row_sub == row_lane, jnp.broadcast_to(delta[pl.ds(source, 1)], (ROWS, WIDTH)), 0.0
        ).astype(jnp.bfloat16)
        first = pl.ds(pl.multiple_of(place * KEY_TOKENS + core * HALF, HALF), HALF)
        second = pl.ds(pl.multiple_of(place * KEY_TOKENS + (1 - core) * HALF, HALF), HALF)
        key[first, 0:WIDTH] = moved[source, 2 * ROWS : 2 * ROWS + HALF]
        key[second, 0:WIDTH] = other_half[source, 0:HALF]
        value[first, 0:WIDTH] = moved[source, 2 * ROWS + HALF : 2 * ROWS + 2 * HALF]
        value[second, 0:WIDTH] = other_half[source, HALF : 2 * HALF]
        return carry

    lax.fori_loop(0, PLACES, sort, 0)
    key_total[...] = jnp.zeros_like(key_total)
    value_total[...] = jnp.zeros_like(value_total)

    def per_row_tile(i, carry):
        here = tile_at(i)
        chosen = jnp.logical_and(lane % TILES == i, lane < 3 * TILES)
        query[here, WIDTH:] = jnp.where(chosen, logs[...], 0.0).astype(jnp.bfloat16)
        query_turned[...] = query[here, 0:WIDTH].T
        grad_turned[...] = grad[here, 0:WIDTH].T
        query_total[...] = jnp.zeros_like(query_total)

        def tile(j, allowed):
            there = tile_at(j)
            probs = jnp.exp2(contract(query[here], key[there], 1, 1) * TO_LOG2)
            if allowed is not None:
                probs = jnp.where(allowed, probs, 0.0)
            moved_probs = contract(grad[here], value[there], 1, 1)
            dscores = (probs * moved_probs).astype(jnp.bfloat16)
            probs_low = probs.astype(jnp.bfloat16)
            value_total[:, there] += contract(grad_turned[...], probs_low, 1, 0)
            key_total[:, there] += contract(query_turned[...], dscores, 1, 0)
            query_total[...] += contract(dscores, key[there, 0:WIDTH], 1, 0)

        def full_tile(j, inner):
            tile(j, None)
            return inner

        lax.fori_loop(0, i, full_tile, 0)
        tile(i, allowed_on_diagonal(key_group, row_group))

        for k in range(SPAN):
            source = table[i * SPAN + k]
            query_grad[source] = (query_total[k * ROWS : (k + 1) * ROWS] * SCALE).astype(
                jnp.bfloat16
            )
        return carry

    lax.fori_loop(0, TILES, per_row_tile, 0)

    def turn(j, carry):
        there = tile_at(j)
        key_sorted[there] = key_total[:, there].T * SCALE
        value_sorted[there] = value_total[:, there].T
        return carry

    lax.fori_loop(0, TILES, turn, 0)

    def unsort(place, carry):
        source = table[place]
        first = pl.ds(pl.multiple_of(place * KEY_TOKENS + core * HALF, HALF), HALF)
        second = pl.ds(pl.multiple_of(place * KEY_TOKENS + (1 - core) * HALF, HALF), HALF)
        own_grad[source, 0:HALF] = key_sorted[first].astype(jnp.bfloat16)
        own_grad[source, HALF:] = value_sorted[first].astype(jnp.bfloat16)
        other_grad[source, 0:HALF] = key_sorted[second].astype(jnp.bfloat16)
        other_grad[source, HALF:] = value_sorted[second].astype(jnp.bfloat16)
        return carry

    lax.fori_loop(0, PLACES, unsort, 0)


IN_VMEM = pl.BlockSpec(memory_space=pltpu.VMEM)
IN_SMEM = pl.BlockSpec(memory_space=pltpu.SMEM)
PAIRS = TILE * TILE * TILES * (TILES + 1) // 2


def stats_call(table, moved, other_half):
    return pl.pallas_call(
        stats_kernel,
        out_shape=jax.ShapeDtypeStruct((2 * TILES, TILE), jnp.float32),
        in_specs=[IN_SMEM, IN_VMEM, IN_VMEM],
        out_specs=IN_VMEM,
        scratch_shapes=[
            pltpu.VMEM((ALL_ROWS, WIDTH), jnp.bfloat16),
            pltpu.VMEM((ALL_KEYS, WIDTH), jnp.bfloat16),
            pltpu.VMEM((TILE, WIDTH), jnp.float32),
            pltpu.VMEM((TILE, WIDTH), jnp.float32),
        ],
        compiler_params=pltpu.CompilerParams(vmem_limit_bytes=VMEM),
        cost_estimate=pl.CostEstimate(
            flops=2 * PAIRS * WIDTH, bytes_accessed=4 << 20, transcendentals=PAIRS
        ),
        name="softmax_totals",
    )(table, moved, other_half)


def gradient_call(table, moved, other_half, delta, stats):
    chunk = jax.ShapeDtypeStruct((PLACES, ROWS, WIDTH), jnp.bfloat16)
    return pl.pallas_call(
        gradient_kernel,
        out_shape=(chunk, chunk, chunk),
        in_specs=[IN_SMEM] + [IN_VMEM] * 7,
        out_specs=(IN_VMEM,) * 3,
        scratch_shapes=[
            pltpu.VMEM((ALL_ROWS, 2 * WIDTH), jnp.bfloat16),
            pltpu.VMEM((ALL_ROWS, 2 * WIDTH), jnp.bfloat16),
            pltpu.VMEM((ALL_KEYS, 2 * WIDTH), jnp.bfloat16),
            pltpu.VMEM((ALL_KEYS, 2 * WIDTH), jnp.bfloat16),
            pltpu.VMEM((WIDTH, TILE), jnp.bfloat16),
            pltpu.VMEM((WIDTH, TILE), jnp.bfloat16),
            pltpu.VMEM((TILE, WIDTH), jnp.float32),
            pltpu.VMEM((TILE, WIDTH), jnp.float32),
            pltpu.VMEM((WIDTH, ALL_KEYS), jnp.float32),
            pltpu.VMEM((WIDTH, ALL_KEYS), jnp.float32),
            pltpu.VMEM((ALL_KEYS, WIDTH), jnp.float32),
            pltpu.VMEM((ALL_KEYS, WIDTH), jnp.float32),
        ],
        compiler_params=pltpu.CompilerParams(vmem_limit_bytes=VMEM),
        cost_estimate=pl.CostEstimate(
            flops=10 * PAIRS * WIDTH, bytes_accessed=8 << 20, transcendentals=PAIRS
        ),
        name="gradients",
    )(table, moved, other_half, delta, *stats)


def shards(queries, key_states, value_states, out_grad, forward_out, stretch_order):
    me = lax.axis_index(ALL)
    swap = [(d, d ^ 1) for d in range(DEVICES)]

    def around(step):
        return [(d, (d + step * ROW_GROUPS) % DEVICES) for d in range(DEVICES)]

    with jax.named_scope("outgoing"):
        products = out_grad.astype(jnp.float32) * forward_out.astype(jnp.float32)
        delta = jnp.sum(products.reshape(STRETCH, HEADS, WIDTH), axis=2).astype(jnp.bfloat16)
        delta = jnp.pad(delta.reshape(ROW_GROUPS, 1, ROWS), ((0, 0), (0, 7), (0, WIDTH - ROWS)))
        by_row_group = jnp.concatenate(
            [
                queries.reshape(ROW_GROUPS, ROWS, WIDTH),
                out_grad.reshape(ROW_GROUPS, ROWS, WIDTH),
            ],
            axis=1,
        )
        by_key_part = jnp.concatenate(
            [
                key_states.reshape(KEY_GROUPS, 1, 2, HALF, WIDTH),
                value_states.reshape(KEY_GROUPS, 1, 2, HALF, WIDTH),
            ],
            axis=3,
        )
        spread = (KEY_GROUPS, ROW_GROUPS // 2, 2, 2 * HALF, WIDTH)
        outgoing = jnp.concatenate(
            [
                jnp.tile(by_row_group, (KEY_GROUPS, 1, 1)),
                jnp.broadcast_to(by_key_part, spread).reshape(DEVICES, 2 * HALF, WIDTH),
                jnp.tile(delta, (KEY_GROUPS, 1, 1)),
            ],
            axis=1,
        )
    with jax.named_scope("exchange_in"):
        moved = lax.all_to_all(outgoing, ALL, split_axis=0, concat_axis=0, tiled=True)
        other_half = lax.ppermute(moved[:, 2 * ROWS : 2 * ROWS + 2 * HALF], ALL, swap)
    with jax.named_scope("table"):
        places = jnp.arange(PLACES, dtype=jnp.int32)
        holder = jnp.sum(
            jnp.where(stretch_order[None, :] == places[:, None], places[None, :], 0), axis=1
        )
        ids = jnp.stack([me // ROW_GROUPS, me % ROW_GROUPS, me % 2]).astype(jnp.int32)
        table = jnp.concatenate([holder, ids])
        delta_in = moved[:, 2 * ROWS + 2 * HALF, :].astype(jnp.float32)
    with jax.named_scope("totals"):
        stats = stats_call(table, moved, other_half)
        all_stats = [stats] + [lax.ppermute(stats, ALL, around(k)) for k in range(1, KEY_GROUPS)]
    with jax.named_scope("gradients"):
        query_grad, own_grad, other_grad = gradient_call(
            table, moved, other_half, delta_in, all_stats
        )
    with jax.named_scope("exchange_out"):
        received = lax.ppermute(other_grad, ALL, swap)
        pair_grad = (own_grad.astype(jnp.float32) + received.astype(jnp.float32)).astype(
            jnp.bfloat16
        )
        back = lax.all_to_all(
            jnp.concatenate([query_grad, pair_grad], axis=1),
            ALL,
            split_axis=0,
            concat_axis=0,
            tiled=True,
        ).astype(jnp.float32)
    with jax.named_scope("sums"):
        d_query = jnp.sum(
            back[:, 0:ROWS].reshape(KEY_GROUPS, ROW_GROUPS, ROWS, WIDTH), axis=0
        ).reshape(STRETCH, HEADS * WIDTH)
        d_pair = jnp.sum(
            back[:, ROWS:].reshape(KEY_GROUPS, ROW_GROUPS // 2, 2, 2, HALF, WIDTH), axis=1
        )
        d_key = d_pair[:, :, 0].reshape(STRETCH, WIDTH)
        d_value = d_pair[:, :, 1].reshape(STRETCH, WIDTH)
    return tuple(part.astype(jnp.bfloat16) for part in (d_query, d_key, d_value))


def solution(mesh):
    split = P(ALL, None)
    return jax.shard_map(
        shards,
        mesh=mesh,
        in_specs=(split,) * 5 + (P(),),
        out_specs=(split,) * 3,
        check_vma=False,
    )
```

```python
import jax
import jax.numpy as jnp
from jax import lax
from jax.experimental import pallas as pl
from jax.experimental.pallas import tpu as pltpu
from jax.sharding import PartitionSpec as P

ALL = ("qrow", "kcol")
DEVICES = 128
HEADS = 8
WIDTH = 128
STRETCH = 128
PLACES = 128
KEY_GROUPS = 4
ROW_GROUPS = 32
QUERY_TOKENS = 16
TOKEN_GROUPS = STRETCH // QUERY_TOKENS
PAIR = 2
HEAD_GROUPS = HEADS // PAIR
KEY_TOKENS = STRETCH // KEY_GROUPS
HALF = KEY_TOKENS // 2
ROWS = QUERY_TOKENS * PAIR
ALL_ROWS = PLACES * ROWS
ALL_KEYS = PLACES * KEY_TOKENS
TILE = 512
TILES = ALL_ROWS // TILE
SPAN = TILE // ROWS
SUBLANES = 8
BIG = 4096
WIDE = 512
BLOCK = 512
SKEW = 2
PART = 512
PARTS = 2 * TILE // PART
CHUNK = 128
NEGATIVE = -1e30
SCALE = float(WIDTH) ** (-0.5)
TO_LOG2 = SCALE * 1.4426950408889634
VMEM = 56 * 1024 * 1024


def contract(left, right, left_dim, right_dim):
    return lax.dot_general(
        left, right, (((left_dim,), (right_dim,)), ((), ())), preferred_element_type=jnp.float32
    )


def tile_at(index):
    return pl.ds(pl.multiple_of(index * TILE, TILE), TILE)


def allowed_on_diagonal(key_group, row_group, row_dim):
    row = lax.broadcasted_iota(jnp.int32, (TILE, TILE), row_dim)
    column = lax.broadcasted_iota(jnp.int32, (TILE, TILE), 1 - row_dim)
    first_token = (row_group // HEAD_GROUPS) * QUERY_TOKENS
    row_place = (row // ROWS) * STRETCH + first_token + row % QUERY_TOKENS
    key_place = (column // KEY_TOKENS) * STRETCH + key_group * KEY_TOKENS + column % KEY_TOKENS
    return key_place <= row_place


def stats_kernel(table, scored, other_key, stats, query, key):
    key_group, row_group, core = table[PLACES], table[PLACES + 1], table[PLACES + 2]

    def sort(place, carry):
        source = table[place]
        query[pl.ds(pl.multiple_of(place * ROWS, ROWS), ROWS)] = scored[source, 0:ROWS]
        first = pl.multiple_of(place * KEY_TOKENS + core * HALF, HALF)
        second = pl.multiple_of(place * KEY_TOKENS + (1 - core) * HALF, HALF)
        key[pl.ds(first, HALF)] = scored[source, ROWS : ROWS + HALF]
        key[pl.ds(second, HALF)] = other_key[source]
        return carry

    lax.fori_loop(0, PLACES, sort, 0, unroll=8)

    def absorb(keys, rows, state, allowed):
        scores = contract(keys, rows, 1, 1)
        if allowed is not None:
            scores = jnp.where(allowed, scores, NEGATIVE)
        highest, summed = state
        scores = scores.reshape(keys.shape[0] // SUBLANES, SUBLANES, rows.shape[0])
        raised = jnp.maximum(highest, jnp.max(scores, axis=0))
        summed = summed * jnp.exp2((highest - raised) * TO_LOG2)
        return raised, summed + jnp.sum(jnp.exp2((scores - raised[None]) * TO_LOG2), axis=0)

    allowed = allowed_on_diagonal(key_group, row_group, 1)
    def per_row_pair(i, carry):
        rows = [
            query[pl.ds(pl.multiple_of(i * 2 * TILE + k * PART, PART), PART)] for k in range(PARTS)
        ]

        def keys_at(j, n):
            return key[pl.ds(pl.multiple_of(j * TILE + n * CHUNK, CHUNK), CHUNK)]

        def full_tile(j, state):
            state = list(state)
            for n in range(TILE // CHUNK):
                keys = keys_at(j, n)
                for k in range(PARTS):
                    state[k] = absorb(keys, rows[k], state[k], None)
            return tuple(state)

        start = (
            jnp.full((SUBLANES, PART), NEGATIVE, jnp.float32),
            jnp.zeros((SUBLANES, PART), jnp.float32),
        )
        state = list(lax.fori_loop(0, 2 * i, full_tile, (start,) * PARTS))
        for n in range(TILE // CHUNK):
            keys = keys_at(2 * i, n)
            for k in range(PARTS):
                mask = None
                if k < PARTS // 2:
                    mask = allowed[n * CHUNK : (n + 1) * CHUNK, k * PART : (k + 1) * PART]
                state[k] = absorb(keys, rows[k], state[k], mask)
            keys = keys_at(2 * i + 1, n)
            for k in range(PARTS // 2):
                mask = allowed[n * CHUNK : (n + 1) * CHUNK, k * PART : (k + 1) * PART]
                late = k + PARTS // 2
                state[late] = absorb(keys, rows[late], state[late], mask)
        for k in range(PARTS):
            highest, summed = state[k]
            row_peak = jnp.max(highest, axis=0, keepdims=True)
            row_total = jnp.sum(
                summed * jnp.exp2((highest - row_peak) * TO_LOG2), axis=0, keepdims=True
            )
            tile = 2 * i + k // (PARTS // 2)
            lanes = (k % (PARTS // 2)) * PART
            stats[pl.ds(tile, 1), lanes : lanes + PART] = row_peak
            stats[pl.ds(tile + TILES, 1), lanes : lanes + PART] = row_total
        return carry

    lax.fori_loop(0, TILES // 2, per_row_pair, 0)


def gradient_kernel(
    table,
    scored,
    other_key,
    weighed,
    other_value,
    delta,
    stats_0,
    stats_1,
    stats_2,
    stats_3,
    own_grad,
    other_grad,
    query,
    grad,
    key,
    value,
    query_turned,
    grad_turned,
    logs,
    query_total,
    key_total,
    value_total,
    key_sorted,
    value_sorted,
):
    key_group, row_group, core = table[PLACES], table[PLACES + 1], table[PLACES + 2]
    lane = lax.broadcasted_iota(jnp.int32, (TILE, WIDTH), 1)
    all_stats = [ref[...] for ref in (stats_0, stats_1, stats_2, stats_3)]
    peaks = [part[0:TILES] for part in all_stats]
    highest = jnp.maximum(jnp.maximum(peaks[0], peaks[1]), jnp.maximum(peaks[2], peaks[3]))
    summed = jnp.zeros_like(highest)
    for part in all_stats:
        summed = summed + part[TILES:] * jnp.exp2((part[0:TILES] - highest) * TO_LOG2)
    log_totals = highest + jnp.log2(summed) * (1.0 / TO_LOG2)
    high = log_totals.astype(jnp.bfloat16).astype(jnp.float32)
    middle = (log_totals - high).astype(jnp.bfloat16).astype(jnp.float32)
    low = (log_totals - high - middle).astype(jnp.bfloat16).astype(jnp.float32)
    padding = jnp.zeros((WIDTH - 3 * TILES, TILE), jnp.float32)
    logs[...] = jnp.concatenate([high, middle, low, padding], axis=0).T

    extra_lane = lax.broadcasted_iota(jnp.int32, (ALL_KEYS, WIDTH), 1)
    key[:, WIDTH:] = jnp.where(extra_lane < 3 * TILES, -1.0, 0.0).astype(jnp.bfloat16)
    value[:, WIDTH:] = jnp.where(extra_lane < ROWS, -1.0, 0.0).astype(jnp.bfloat16)
    row_sub = lax.broadcasted_iota(jnp.int32, (ROWS, WIDTH), 0)
    row_lane = lax.broadcasted_iota(jnp.int32, (ROWS, WIDTH), 1)

    def sort(place, carry):
        source = table[place]
        spot = pl.ds(pl.multiple_of(place * ROWS, ROWS), ROWS)
        query[spot, 0:WIDTH] = scored[source, 0:ROWS]
        grad[spot, 0:WIDTH] = weighed[source, 0:ROWS]
        grad[spot, WIDTH:] = jnp.where(
            row_sub == row_lane, jnp.broadcast_to(delta[pl.ds(source, 1)], (ROWS, WIDTH)), 0.0
        ).astype(jnp.bfloat16)
        first = pl.ds(pl.multiple_of(place * KEY_TOKENS + core * HALF, HALF), HALF)
        second = pl.ds(pl.multiple_of(place * KEY_TOKENS + (1 - core) * HALF, HALF), HALF)
        key[first, 0:WIDTH] = scored[source, ROWS : ROWS + HALF]
        key[second, 0:WIDTH] = other_key[source]
        value[first, 0:WIDTH] = weighed[source, ROWS : ROWS + HALF]
        value[second, 0:WIDTH] = other_value[source]
        return carry

    lax.fori_loop(0, PLACES, sort, 0, unroll=8)
    key_total[...] = jnp.zeros_like(key_total)
    value_total[...] = jnp.zeros_like(value_total)

    allowed = allowed_on_diagonal(key_group, row_group, 0)[0:BLOCK, 0:BLOCK]

    def per_row_tile(i, carry):
        chosen_lanes = lane < 3 * TILES
        for h in range(BIG // TILE):
            here = tile_at(i * (BIG // TILE) + h)
            chosen = jnp.logical_and(lane % TILES == i * (BIG // TILE) + h, chosen_lanes)
            query[here, WIDTH:] = jnp.where(chosen, logs[...], 0.0).astype(jnp.bfloat16)
            query_turned[:, h * TILE : (h + 1) * TILE] = query[here, 0:WIDTH].T
            grad_turned[:, h * TILE : (h + 1) * TILE] = grad[here, 0:WIDTH].T
        query_total[...] = jnp.zeros_like(query_total)

        def rows_at(r):
            return pl.ds(pl.multiple_of(i * BIG + r * BLOCK, BLOCK), BLOCK)

        def work(keys_at, blocks):
            def first(block):
                r, k, masked = block
                scores = contract(query[rows_at(r)], key[keys_at(k)], 1, 1)
                probs = jnp.exp2(scores * TO_LOG2)
                if masked:
                    probs = jnp.where(allowed, probs, 0.0)
                moved_probs = contract(grad[rows_at(r)], value[keys_at(k)], 1, 1)
                return probs.astype(jnp.bfloat16), (probs * moved_probs).astype(jnp.bfloat16)

            value_sums, key_sums, query_sums = {}, {}, {}

            def add(sums, spot, part):
                sums[spot] = sums[spot] + part if spot in sums else part

            def second(block, probs_low, dscores):
                r, k, _ = block
                span = slice(r * BLOCK, (r + 1) * BLOCK)
                add(value_sums, k, contract(grad_turned[:, span], probs_low, 1, 0))
                add(key_sums, k, contract(query_turned[:, span], dscores, 1, 0))
                add(query_sums, r, contract(dscores, key[keys_at(k), 0:WIDTH], 1, 0))

            waiting = []
            for block in blocks:
                waiting.append((block,) + first(block))
                if len(waiting) > SKEW:
                    second(*waiting.pop(0))
            for entry in waiting:
                second(*entry)
            for k, part in value_sums.items():
                value_total[:, keys_at(k)] += part
            for k, part in key_sums.items():
                key_total[:, keys_at(k)] += part
            for r, part in query_sums.items():
                query_total[r * BLOCK : (r + 1) * BLOCK] += part

        def full_tile(j, inner):
            def keys_at(k):
                return pl.ds(pl.multiple_of(j * WIDE + k * BLOCK, BLOCK), BLOCK)

            work(
                keys_at,
                [(r, k, False) for k in range(WIDE // BLOCK) for r in range(BIG // BLOCK)],
            )
            return inner

        lax.fori_loop(0, i * (BIG // WIDE), full_tile, 0)
        work(
            rows_at,
            [(r, k, r == k) for k in range(BIG // BLOCK) for r in range(k, BIG // BLOCK)],
        )

        for k in range(BIG // ROWS):
            source = table[i * (BIG // ROWS) + k]
            own_grad[source, 0:ROWS] = (query_total[k * ROWS : (k + 1) * ROWS] * SCALE).astype(
                jnp.bfloat16
            )
        return carry

    lax.fori_loop(0, ALL_ROWS // BIG, per_row_tile, 0)

    def turn(j, carry):
        there = tile_at(j)
        key_sorted[there] = key_total[:, there].T * SCALE
        value_sorted[there] = value_total[:, there].T
        return carry

    lax.fori_loop(0, TILES, turn, 0)

    def unsort(place, carry):
        source = table[place]
        first = pl.ds(pl.multiple_of(place * KEY_TOKENS + core * HALF, HALF), HALF)
        second = pl.ds(pl.multiple_of(place * KEY_TOKENS + (1 - core) * HALF, HALF), HALF)
        own_grad[source, ROWS : ROWS + HALF] = key_sorted[first].astype(jnp.bfloat16)
        own_grad[source, ROWS + HALF :] = value_sorted[first].astype(jnp.bfloat16)
        other_grad[source, 0:HALF] = key_sorted[second].astype(jnp.bfloat16)
        other_grad[source, HALF:] = value_sorted[second].astype(jnp.bfloat16)
        return carry

    lax.fori_loop(0, PLACES, unsort, 0, unroll=8)


IN_VMEM = pl.BlockSpec(memory_space=pltpu.VMEM)
IN_SMEM = pl.BlockSpec(memory_space=pltpu.SMEM)
PAIRS = TILE * TILE * TILES * (TILES + 1) // 2


def stats_call(table, scored, other_key):
    return pl.pallas_call(
        stats_kernel,
        out_shape=jax.ShapeDtypeStruct((2 * TILES, TILE), jnp.float32),
        in_specs=[IN_SMEM, IN_VMEM, IN_VMEM],
        out_specs=IN_VMEM,
        scratch_shapes=[
            pltpu.VMEM((ALL_ROWS, WIDTH), jnp.bfloat16),
            pltpu.VMEM((ALL_KEYS, WIDTH), jnp.bfloat16),
        ],
        compiler_params=pltpu.CompilerParams(vmem_limit_bytes=VMEM),
        cost_estimate=pl.CostEstimate(
            flops=2 * PAIRS * WIDTH, bytes_accessed=4 << 20, transcendentals=PAIRS
        ),
        name="softmax_totals",
    )(table, scored, other_key)


def gradient_call(table, scored, other_key, weighed, other_value, delta, stats):
    own = jax.ShapeDtypeStruct((PLACES, ROWS + 2 * HALF, WIDTH), jnp.bfloat16)
    other = jax.ShapeDtypeStruct((PLACES, 2 * HALF, WIDTH), jnp.bfloat16)
    return pl.pallas_call(
        gradient_kernel,
        out_shape=(own, other),
        in_specs=[IN_SMEM] + [IN_VMEM] * 9,
        out_specs=(IN_VMEM,) * 2,
        scratch_shapes=[
            pltpu.VMEM((ALL_ROWS, 2 * WIDTH), jnp.bfloat16),
            pltpu.VMEM((ALL_ROWS, 2 * WIDTH), jnp.bfloat16),
            pltpu.VMEM((ALL_KEYS, 2 * WIDTH), jnp.bfloat16),
            pltpu.VMEM((ALL_KEYS, 2 * WIDTH), jnp.bfloat16),
            pltpu.VMEM((WIDTH, BIG), jnp.bfloat16),
            pltpu.VMEM((WIDTH, BIG), jnp.bfloat16),
            pltpu.VMEM((TILE, WIDTH), jnp.float32),
            pltpu.VMEM((BIG, WIDTH), jnp.float32),
            pltpu.VMEM((WIDTH, ALL_KEYS), jnp.float32),
            pltpu.VMEM((WIDTH, ALL_KEYS), jnp.float32),
            pltpu.VMEM((ALL_KEYS, WIDTH), jnp.float32),
            pltpu.VMEM((ALL_KEYS, WIDTH), jnp.float32),
        ],
        compiler_params=pltpu.CompilerParams(vmem_limit_bytes=VMEM),
        cost_estimate=pl.CostEstimate(
            flops=10 * PAIRS * WIDTH, bytes_accessed=8 << 20, transcendentals=PAIRS
        ),
        name="gradients",
    )(table, scored, other_key, weighed, other_value, delta, *stats)


def pack_kernel(rows, keys, outgoing):
    for r in range(ROW_GROUPS):
        tokens = (r // HEAD_GROUPS) * QUERY_TOKENS
        for h in range(PAIR):
            head = (r % HEAD_GROUPS) * PAIR + h
            part = rows[tokens : tokens + QUERY_TOKENS, head * WIDTH : (head + 1) * WIDTH]
            for g in range(KEY_GROUPS):
                outgoing[
                    g * ROW_GROUPS + r, h * QUERY_TOKENS : (h + 1) * QUERY_TOKENS
                ] = part
    for g in range(KEY_GROUPS):
        for c in range(2):
            first = g * KEY_TOKENS + c * HALF
            part = keys[first : first + HALF]
            for r in range(c, ROW_GROUPS, 2):
                outgoing[g * ROW_GROUPS + r, ROWS : ROWS + HALF] = part


def pack_call(rows, keys):
    return pl.pallas_call(
        pack_kernel,
        out_shape=jax.ShapeDtypeStruct((DEVICES, ROWS + HALF, WIDTH), jnp.bfloat16),
        in_specs=[IN_VMEM] * 2,
        out_specs=IN_VMEM,
        compiler_params=pltpu.CompilerParams(vmem_limit_bytes=VMEM // 4),
        name="pack",
    )(rows, keys)


def pair_kernel(own, received, outgoing):
    outgoing[:, 0:ROWS] = own[:, 0:ROWS]
    total = own[:, ROWS:].astype(jnp.float32) + received[...].astype(jnp.float32)
    outgoing[:, ROWS:] = total.astype(jnp.bfloat16)


def pair_call(own, received):
    return pl.pallas_call(
        pair_kernel,
        out_shape=jax.ShapeDtypeStruct(own.shape, own.dtype),
        in_specs=[IN_VMEM] * 2,
        out_specs=IN_VMEM,
        compiler_params=pltpu.CompilerParams(vmem_limit_bytes=VMEM // 2),
        name="pair_sum",
    )(own, received)


def sums_kernel(back, d_query, d_key, d_value):
    for r in range(ROW_GROUPS):
        total = back[r, 0:ROWS].astype(jnp.float32)
        for g in range(1, KEY_GROUPS):
            total = total + back[g * ROW_GROUPS + r, 0:ROWS].astype(jnp.float32)
        total = total.astype(jnp.bfloat16)
        tokens = (r // HEAD_GROUPS) * QUERY_TOKENS
        for h in range(PAIR):
            head = (r % HEAD_GROUPS) * PAIR + h
            d_query[tokens : tokens + QUERY_TOKENS, head * WIDTH : (head + 1) * WIDTH] = total[
                h * QUERY_TOKENS : (h + 1) * QUERY_TOKENS
            ]
    for g in range(KEY_GROUPS):
        for c in range(2):
            total = jnp.zeros((2 * HALF, WIDTH), jnp.float32)
            for r in range(c, ROW_GROUPS, 2):
                total = total + back[g * ROW_GROUPS + r, ROWS:].astype(jnp.float32)
            first = g * KEY_TOKENS + c * HALF
            d_key[first : first + HALF] = total[0:HALF].astype(jnp.bfloat16)
            d_value[first : first + HALF] = total[HALF:].astype(jnp.bfloat16)


def sums_call(back):
    small = jax.ShapeDtypeStruct((STRETCH, WIDTH), jnp.bfloat16)
    return pl.pallas_call(
        sums_kernel,
        out_shape=(
            jax.ShapeDtypeStruct((STRETCH, HEADS * WIDTH), jnp.bfloat16),
            small,
            small,
        ),
        in_specs=[IN_VMEM],
        out_specs=(IN_VMEM,) * 3,
        compiler_params=pltpu.CompilerParams(vmem_limit_bytes=VMEM // 4),
        name="sums",
    )(back)


def shards(queries, key_states, value_states, out_grad, forward_out, stretch_order):
    me = lax.axis_index(ALL)
    swap = [(d, d ^ 1) for d in range(DEVICES)]

    def around(step):
        return [(d, (d + step * ROW_GROUPS) % DEVICES) for d in range(DEVICES)]

    with jax.named_scope("outgoing"):
        scored = pack_call(queries, key_states)
        products = out_grad.astype(jnp.float32) * forward_out.astype(jnp.float32)
        delta = jnp.sum(products.reshape(STRETCH, HEADS, WIDTH), axis=2).astype(jnp.bfloat16)
        delta = delta.reshape(TOKEN_GROUPS, QUERY_TOKENS, HEAD_GROUPS, PAIR)
        delta = delta.transpose(0, 2, 3, 1).reshape(ROW_GROUPS, 1, ROWS)
        delta = jnp.pad(delta, ((0, 0), (0, 7), (0, WIDTH - ROWS)))
        weighed = jnp.concatenate(
            [pack_call(out_grad, value_states), jnp.tile(delta, (KEY_GROUPS, 1, 1))], axis=1
        )
    with jax.named_scope("table"):
        places = jnp.arange(PLACES, dtype=jnp.int32)
        holder = jnp.sum(
            jnp.where(stretch_order[None, :] == places[:, None], places[None, :], 0), axis=1
        )
        ids = jnp.stack([me // ROW_GROUPS, me % ROW_GROUPS, me % 2]).astype(jnp.int32)
        table = jnp.concatenate([holder, ids])
    with jax.named_scope("exchange_in"):
        scored = lax.all_to_all(scored, ALL, split_axis=0, concat_axis=0, tiled=True)
        weighed = lax.all_to_all(weighed, ALL, split_axis=0, concat_axis=0, tiled=True)
        other_key = lax.ppermute(scored[:, ROWS:], ALL, swap)
    with jax.named_scope("totals"):
        stats = stats_call(table, scored, other_key)
        all_stats = [stats] + [lax.ppermute(stats, ALL, around(k)) for k in range(1, KEY_GROUPS)]
        weighed, *all_stats = lax.optimization_barrier((weighed, *all_stats))
        other_value = lax.ppermute(weighed[:, ROWS : ROWS + HALF], ALL, swap)
        delta_in = weighed[:, ROWS + HALF, :].astype(jnp.float32)
    with jax.named_scope("gradients"):
        own_grad, other_grad = gradient_call(
            table, scored, other_key, weighed, other_value, delta_in, all_stats
        )
    with jax.named_scope("exchange_out"):
        received = lax.ppermute(other_grad, ALL, swap)
        outgoing = pair_call(own_grad, received)
        back = lax.all_to_all(outgoing, ALL, split_axis=0, concat_axis=0, tiled=True)
    with jax.named_scope("sums"):
        return sums_call(back)


def solution(mesh):
    split = P(ALL, None)
    return jax.shard_map(
        shards,
        mesh=mesh,
        in_specs=(split,) * 5 + (P(),),
        out_specs=(split,) * 3,
        check_vma=False,
    )
```

```python
import jax
import jax.numpy as jnp
from jax import lax
from jax.experimental import pallas as pl
from jax.experimental.pallas import tpu as pltpu
from jax.sharding import PartitionSpec as P

ALL = ("qrow", "kcol")
DEVICES = 128
HEADS = 8
WIDTH = 128
STRETCH = 128
PLACES = 128
KEY_GROUPS = 4
ROW_GROUPS = 32
QUERY_TOKENS = 16
TOKEN_GROUPS = STRETCH // QUERY_TOKENS
PAIR = 2
HEAD_GROUPS = HEADS // PAIR
KEY_TOKENS = STRETCH // KEY_GROUPS
HALF = KEY_TOKENS // 2
ROWS = QUERY_TOKENS * PAIR
ALL_ROWS = PLACES * ROWS
ALL_KEYS = PLACES * KEY_TOKENS
TILE = 512
TILES = ALL_ROWS // TILE
SPAN = TILE // ROWS
SUBLANES = 8
SKEW = 2
PART = 512
PARTS = 2 * TILE // PART
CHUNK = 128
NEGATIVE = -1e30
SCALE = float(WIDTH) ** (-0.5)
TO_LOG2 = SCALE * 1.4426950408889634
MIB = 1024 * 1024


def contract(left, right, left_dim, right_dim):
    return lax.dot_general(
        left, right, (((left_dim,), (right_dim,)), ((), ())), preferred_element_type=jnp.float32
    )


def tile_at(index):
    return pl.ds(pl.multiple_of(index * TILE, TILE), TILE)


def allowed_on_diagonal(key_group, row_group, row_dim):
    row = lax.broadcasted_iota(jnp.int32, (TILE, TILE), row_dim)
    column = lax.broadcasted_iota(jnp.int32, (TILE, TILE), 1 - row_dim)
    first_token = (row_group // HEAD_GROUPS) * QUERY_TOKENS
    row_place = (row // ROWS) * STRETCH + first_token + row % QUERY_TOKENS
    key_place = (column // KEY_TOKENS) * STRETCH + key_group * KEY_TOKENS + column % KEY_TOKENS
    return key_place <= row_place


def stats_kernel(table, scored, other_half, stats, query, key):
    key_group, row_group, core = table[PLACES], table[PLACES + 1], table[PLACES + 2]

    def sort(place, carry):
        source = table[place]
        query[pl.ds(pl.multiple_of(place * ROWS, ROWS), ROWS)] = scored[source, 0:ROWS]
        first = pl.multiple_of(place * KEY_TOKENS + core * HALF, HALF)
        second = pl.multiple_of(place * KEY_TOKENS + (1 - core) * HALF, HALF)
        key[pl.ds(first, HALF)] = scored[source, ROWS : ROWS + HALF]
        key[pl.ds(second, HALF)] = other_half[source, 0:HALF]
        return carry

    lax.fori_loop(0, PLACES, sort, 0, unroll=8)

    def absorb(keys, rows, state, allowed):
        scores = contract(keys, rows, 1, 1)
        if allowed is not None:
            scores = jnp.where(allowed, scores, NEGATIVE)
        highest, summed = state
        scores = scores.reshape(keys.shape[0] // SUBLANES, SUBLANES, rows.shape[0])
        raised = jnp.maximum(highest, jnp.max(scores, axis=0))
        summed = summed * jnp.exp2((highest - raised) * TO_LOG2)
        return raised, summed + jnp.sum(jnp.exp2((scores - raised[None]) * TO_LOG2), axis=0)

    allowed = allowed_on_diagonal(key_group, row_group, 1)
    def per_row_pair(i, carry):
        rows = [
            query[pl.ds(pl.multiple_of(i * 2 * TILE + k * PART, PART), PART)] for k in range(PARTS)
        ]

        def keys_at(j, n):
            return key[pl.ds(pl.multiple_of(j * TILE + n * CHUNK, CHUNK), CHUNK)]

        def full_tile(j, state):
            state = list(state)
            for n in range(TILE // CHUNK):
                keys = keys_at(j, n)
                for k in range(PARTS):
                    state[k] = absorb(keys, rows[k], state[k], None)
            return tuple(state)

        start = (
            jnp.full((SUBLANES, PART), NEGATIVE, jnp.float32),
            jnp.zeros((SUBLANES, PART), jnp.float32),
        )
        state = list(lax.fori_loop(0, 2 * i, full_tile, (start,) * PARTS))
        for n in range(TILE // CHUNK):
            keys = keys_at(2 * i, n)
            for k in range(PARTS):
                mask = None
                if k < PARTS // 2:
                    mask = allowed[n * CHUNK : (n + 1) * CHUNK, k * PART : (k + 1) * PART]
                state[k] = absorb(keys, rows[k], state[k], mask)
            keys = keys_at(2 * i + 1, n)
            for k in range(PARTS // 2):
                mask = allowed[n * CHUNK : (n + 1) * CHUNK, k * PART : (k + 1) * PART]
                late = k + PARTS // 2
                state[late] = absorb(keys, rows[late], state[late], mask)
        for k in range(PARTS):
            highest, summed = state[k]
            row_peak = jnp.max(highest, axis=0, keepdims=True)
            row_total = jnp.sum(
                summed * jnp.exp2((highest - row_peak) * TO_LOG2), axis=0, keepdims=True
            )
            tile = 2 * i + k // (PARTS // 2)
            lanes = (k % (PARTS // 2)) * PART
            stats[pl.ds(tile, 1), lanes : lanes + PART] = row_peak
            stats[pl.ds(tile + TILES, 1), lanes : lanes + PART] = row_total
        return carry

    lax.fori_loop(0, TILES // 2, per_row_pair, 0)


def gradient_kernel(
    table,
    scored,
    other_half,
    weighed,
    stats_0,
    stats_1,
    stats_2,
    stats_3,
    own_grad,
    other_grad,
    query,
    grad,
    query_turned,
    grad_turned,
    key,
    value,
    logs,
    key_sorted,
    value_sorted,
):
    key_group, row_group, core = table[PLACES], table[PLACES + 1], table[PLACES + 2]
    lane = lax.broadcasted_iota(jnp.int32, (TILE, WIDTH), 1)
    row_token = lax.broadcasted_iota(jnp.int32, (ROWS, WIDTH), 0) % QUERY_TOKENS
    row_token = row_token + (row_group // HEAD_GROUPS) * QUERY_TOKENS
    own_lane = lax.broadcasted_iota(jnp.int32, (ROWS, WIDTH), 1) == row_token
    all_stats = [ref[...] for ref in (stats_0, stats_1, stats_2, stats_3)]
    peaks = [part[0:TILES] for part in all_stats]
    highest = jnp.maximum(jnp.maximum(peaks[0], peaks[1]), jnp.maximum(peaks[2], peaks[3]))
    summed = jnp.zeros_like(highest)
    for part in all_stats:
        summed = summed + part[TILES:] * jnp.exp2((part[0:TILES] - highest) * TO_LOG2)
    log_totals = highest + jnp.log2(summed) * (1.0 / TO_LOG2)
    high = log_totals.astype(jnp.bfloat16).astype(jnp.float32)
    middle = (log_totals - high).astype(jnp.bfloat16).astype(jnp.float32)
    low = (log_totals - high - middle).astype(jnp.bfloat16).astype(jnp.float32)
    padding = jnp.zeros((WIDTH - 3 * TILES, TILE), jnp.float32)
    logs[...] = jnp.concatenate([high, middle, low, padding], axis=0).T
    allowed = allowed_on_diagonal(key_group, row_group, 0)
    key_extra = jnp.where(lane < 3 * TILES, -1.0, 0.0).astype(jnp.bfloat16)
    value_extra = jnp.full((TILE, WIDTH), -1.0, jnp.bfloat16)

    def tile_span(t):
        return slice(t * TILE, (t + 1) * TILE)

    def prepare_rows(r):
        here = tile_span(r)
        chosen = jnp.logical_and(lane % TILES == r, lane < 3 * TILES)
        query[here, WIDTH:] = jnp.where(chosen, logs[...], 0.0).astype(jnp.bfloat16)
        for k in range(SPAN):
            source = table[r * SPAN + k]
            spot = slice(r * TILE + k * ROWS, r * TILE + (k + 1) * ROWS)
            query[spot, 0:WIDTH] = scored[source, 0:ROWS]
            grad[spot, 0:WIDTH] = weighed[source, 0:ROWS]
            delta = weighed[source, ROWS : ROWS + SUBLANES].astype(jnp.float32)
            per_row = [
                jnp.broadcast_to(delta[h : h + 1], (QUERY_TOKENS, WIDTH)) for h in range(PAIR)
            ]
            grad[spot, WIDTH:] = jnp.where(own_lane, jnp.concatenate(per_row, axis=0), 0.0).astype(
                jnp.bfloat16
            )
        query_turned[:, here] = query[here, 0:WIDTH].T
        grad_turned[:, here] = grad[here, 0:WIDTH].T

    def prepare_keys(k):
        here = tile_span(k)
        key[here, WIDTH:] = key_extra
        value[here, WIDTH:] = value_extra
        for s in range(SPAN):
            source = table[k * SPAN + s]
            start = k * TILE + s * KEY_TOKENS
            own_spot = pl.ds(pl.multiple_of(start + core * HALF, HALF), HALF)
            other_spot = pl.ds(pl.multiple_of(start + (1 - core) * HALF, HALF), HALF)
            key[own_spot, 0:WIDTH] = scored[source, ROWS : ROWS + HALF]
            key[other_spot, 0:WIDTH] = other_half[source, 0:HALF]
            value[own_spot, 0:WIDTH] = scored[source, ROWS + HALF : ROWS + 2 * HALF]
            value[other_spot, 0:WIDTH] = other_half[source, HALF : 2 * HALF]

    def first(r, k):
        scores = contract(query[tile_span(r)], key[tile_span(k)], 1, 1)
        probs = jnp.exp2(scores * TO_LOG2)
        if r == k:
            probs = jnp.where(allowed, probs, 0.0)
        moved_probs = contract(grad[tile_span(r)], value[tile_span(k)], 1, 1)
        return probs.astype(jnp.bfloat16), (probs * moved_probs).astype(jnp.bfloat16)

    value_sums, key_sums, query_sums = {}, {}, {}

    def add(sums, spot, part):
        sums[spot] = sums[spot] + part if spot in sums else part

    def second(r, k, probs_low, dscores):
        add(value_sums, k, contract(grad_turned[:, tile_span(r)], probs_low, 1, 0))
        add(key_sums, k, contract(query_turned[:, tile_span(r)], dscores, 1, 0))
        add(query_sums, r, contract(dscores, key[tile_span(k), 0:WIDTH], 1, 0))
        if r == k:
            total = (query_sums.pop(r) * SCALE).astype(jnp.bfloat16)
            for s in range(SPAN):
                own_grad[table[r * SPAN + s], 0:ROWS] = total[s * ROWS : (s + 1) * ROWS]
        if r == TILES - 1:
            key_part = (key_sums.pop(k) * SCALE).astype(jnp.bfloat16).T
            value_part = value_sums.pop(k).astype(jnp.bfloat16).T
            key_sorted[tile_span(k)] = key_part
            value_sorted[tile_span(k)] = value_part

    waiting = []
    for k in range(TILES):
        prepare_keys(k)
        for r in range(k, TILES):
            if k == 0:
                prepare_rows(r)
            waiting.append((r, k) + first(r, k))
            if len(waiting) > SKEW:
                second(*waiting.pop(0))
    for entry in waiting:
        second(*entry)

    def unsort(place, carry):
        source = table[place]
        first = pl.ds(pl.multiple_of(place * KEY_TOKENS + core * HALF, HALF), HALF)
        second = pl.ds(pl.multiple_of(place * KEY_TOKENS + (1 - core) * HALF, HALF), HALF)
        own_grad[source, ROWS : ROWS + HALF] = key_sorted[first]
        own_grad[source, ROWS + HALF :] = value_sorted[first]
        other_grad[source, 0:HALF] = key_sorted[second]
        other_grad[source, HALF:] = value_sorted[second]
        return carry

    lax.fori_loop(0, PLACES, unsort, 0, unroll=8)


IN_VMEM = pl.BlockSpec(memory_space=pltpu.VMEM)
IN_SMEM = pl.BlockSpec(memory_space=pltpu.SMEM)
PAIRS = TILE * TILE * TILES * (TILES + 1) // 2


def stats_call(table, scored, other_half):
    return pl.pallas_call(
        stats_kernel,
        out_shape=jax.ShapeDtypeStruct((2 * TILES, TILE), jnp.float32),
        in_specs=[IN_SMEM, IN_VMEM, IN_VMEM],
        out_specs=IN_VMEM,
        scratch_shapes=[
            pltpu.VMEM((ALL_ROWS, WIDTH), jnp.bfloat16),
            pltpu.VMEM((ALL_KEYS, WIDTH), jnp.bfloat16),
        ],
        compiler_params=pltpu.CompilerParams(vmem_limit_bytes=20 * MIB),
        cost_estimate=pl.CostEstimate(
            flops=2 * PAIRS * WIDTH, bytes_accessed=4 * MIB, transcendentals=PAIRS
        ),
        name="softmax_totals",
    )(table, scored, other_half)


def gradient_call(table, scored, other_half, weighed, stats):
    own = jax.ShapeDtypeStruct((PLACES, ROWS + 2 * HALF, WIDTH), jnp.bfloat16)
    other = jax.ShapeDtypeStruct((PLACES, 2 * HALF, WIDTH), jnp.bfloat16)
    return pl.pallas_call(
        gradient_kernel,
        out_shape=(own, other),
        in_specs=[IN_SMEM] + [IN_VMEM] * 7,
        out_specs=(IN_VMEM,) * 2,
        scratch_shapes=[
            pltpu.VMEM((ALL_ROWS, 2 * WIDTH), jnp.bfloat16),
            pltpu.VMEM((ALL_ROWS, 2 * WIDTH), jnp.bfloat16),
            pltpu.VMEM((WIDTH, ALL_ROWS), jnp.bfloat16),
            pltpu.VMEM((WIDTH, ALL_ROWS), jnp.bfloat16),
            pltpu.VMEM((ALL_KEYS, 2 * WIDTH), jnp.bfloat16),
            pltpu.VMEM((ALL_KEYS, 2 * WIDTH), jnp.bfloat16),
            pltpu.VMEM((TILE, WIDTH), jnp.float32),
            pltpu.VMEM((ALL_KEYS, WIDTH), jnp.bfloat16),
            pltpu.VMEM((ALL_KEYS, WIDTH), jnp.bfloat16),
        ],
        compiler_params=pltpu.CompilerParams(vmem_limit_bytes=32 * MIB),
        cost_estimate=pl.CostEstimate(
            flops=10 * PAIRS * WIDTH, bytes_accessed=8 * MIB, transcendentals=PAIRS
        ),
        name="gradients",
    )(table, scored, other_half, weighed, *stats)


def pack_rows(rows, outgoing):
    for r in range(ROW_GROUPS):
        tokens = (r // HEAD_GROUPS) * QUERY_TOKENS
        for h in range(PAIR):
            head = (r % HEAD_GROUPS) * PAIR + h
            part = rows[tokens : tokens + QUERY_TOKENS, head * WIDTH : (head + 1) * WIDTH]
            for g in range(KEY_GROUPS):
                outgoing[
                    g * ROW_GROUPS + r, h * QUERY_TOKENS : (h + 1) * QUERY_TOKENS
                ] = part


def pack_kernel(rows, keys, values, outgoing):
    pack_rows(rows, outgoing)
    for g in range(KEY_GROUPS):
        for c in range(2):
            first = g * KEY_TOKENS + c * HALF
            for n, array in enumerate((keys, values)):
                part = array[first : first + HALF]
                spot = slice(ROWS + n * HALF, ROWS + (n + 1) * HALF)
                for r in range(c, ROW_GROUPS, 2):
                    outgoing[g * ROW_GROUPS + r, spot] = part


def pack_grad_kernel(rows, forward, outgoing):
    pack_rows(rows, outgoing)
    lane = lax.broadcasted_iota(jnp.int32, (STRETCH, WIDTH), 1)
    delta = jnp.zeros((STRETCH, WIDTH), jnp.float32)
    for head in range(HEADS):
        span = slice(head * WIDTH, (head + 1) * WIDTH)
        products = rows[:, span].astype(jnp.float32) * forward[:, span].astype(jnp.float32)
        delta = jnp.where(lane == head, jnp.sum(products, axis=1, keepdims=True), delta)
    delta = delta.T
    blank = jnp.zeros((SUBLANES - PAIR, WIDTH), jnp.float32)
    for p in range(HEAD_GROUPS):
        part = jnp.concatenate([delta[PAIR * p : PAIR * (p + 1)], blank], axis=0)
        part = part.astype(jnp.bfloat16)
        for r in range(p, DEVICES, HEAD_GROUPS):
            outgoing[r, ROWS : ROWS + SUBLANES] = part


def pack_call(kernel, height, *arrays):
    return pl.pallas_call(
        kernel,
        out_shape=jax.ShapeDtypeStruct((DEVICES, height, WIDTH), jnp.bfloat16),
        in_specs=[IN_VMEM] * len(arrays),
        out_specs=IN_VMEM,
        compiler_params=pltpu.CompilerParams(vmem_limit_bytes=56 * MIB),
        name="pack",
    )(*arrays)


def pair_kernel(own, received, outgoing):
    outgoing[:, 0:ROWS] = own[:, 0:ROWS]
    total = own[:, ROWS:].astype(jnp.float32) + received[...].astype(jnp.float32)
    outgoing[:, ROWS:] = total.astype(jnp.bfloat16)


def pair_call(own, received):
    return pl.pallas_call(
        pair_kernel,
        out_shape=jax.ShapeDtypeStruct(own.shape, own.dtype),
        in_specs=[IN_VMEM] * 2,
        out_specs=IN_VMEM,
        compiler_params=pltpu.CompilerParams(vmem_limit_bytes=16 * MIB),
        name="pair_sum",
    )(own, received)


def sums_kernel(back, d_query, d_key, d_value):
    for r in range(ROW_GROUPS):
        total = back[r, 0:ROWS].astype(jnp.float32)
        for g in range(1, KEY_GROUPS):
            total = total + back[g * ROW_GROUPS + r, 0:ROWS].astype(jnp.float32)
        total = total.astype(jnp.bfloat16)
        tokens = (r // HEAD_GROUPS) * QUERY_TOKENS
        for h in range(PAIR):
            head = (r % HEAD_GROUPS) * PAIR + h
            d_query[tokens : tokens + QUERY_TOKENS, head * WIDTH : (head + 1) * WIDTH] = total[
                h * QUERY_TOKENS : (h + 1) * QUERY_TOKENS
            ]
    for g in range(KEY_GROUPS):
        for c in range(2):
            total = jnp.zeros((2 * HALF, WIDTH), jnp.float32)
            for r in range(c, ROW_GROUPS, 2):
                total = total + back[g * ROW_GROUPS + r, ROWS:].astype(jnp.float32)
            first = g * KEY_TOKENS + c * HALF
            d_key[first : first + HALF] = total[0:HALF].astype(jnp.bfloat16)
            d_value[first : first + HALF] = total[HALF:].astype(jnp.bfloat16)


def sums_call(back):
    small = jax.ShapeDtypeStruct((STRETCH, WIDTH), jnp.bfloat16)
    return pl.pallas_call(
        sums_kernel,
        out_shape=(
            jax.ShapeDtypeStruct((STRETCH, HEADS * WIDTH), jnp.bfloat16),
            small,
            small,
        ),
        in_specs=[IN_VMEM],
        out_specs=(IN_VMEM,) * 3,
        compiler_params=pltpu.CompilerParams(vmem_limit_bytes=12 * MIB),
        name="sums",
    )(back)


def shards(queries, key_states, value_states, out_grad, forward_out, stretch_order):
    me = lax.axis_index(ALL)
    swap = [(d, d ^ 1) for d in range(DEVICES)]

    def around(step):
        return [(d, (d + step * ROW_GROUPS) % DEVICES) for d in range(DEVICES)]

    with jax.named_scope("outgoing"):
        scored = pack_call(pack_kernel, ROWS + 2 * HALF, queries, key_states, value_states)
        weighed = pack_call(pack_grad_kernel, ROWS + SUBLANES, out_grad, forward_out)
    with jax.named_scope("table"):
        places = jnp.arange(PLACES, dtype=jnp.int32)
        holder = jnp.sum(
            jnp.where(stretch_order[None, :] == places[:, None], places[None, :], 0), axis=1
        )
        ids = jnp.stack([me // ROW_GROUPS, me % ROW_GROUPS, me % 2]).astype(jnp.int32)
        table = jnp.concatenate([holder, ids])
    with jax.named_scope("exchange_in"):
        scored = lax.all_to_all(scored, ALL, split_axis=0, concat_axis=0, tiled=True)
        scored, weighed = lax.optimization_barrier((scored, weighed))
        weighed = lax.all_to_all(weighed, ALL, split_axis=0, concat_axis=0, tiled=True)
        other_half = lax.ppermute(scored[:, ROWS:], ALL, swap)
    with jax.named_scope("totals"):
        stats = stats_call(table, scored, other_half)
        all_stats = [stats] + [lax.ppermute(stats, ALL, around(k)) for k in range(1, KEY_GROUPS)]
        weighed, all_stats = lax.optimization_barrier((weighed, all_stats))
    with jax.named_scope("gradients"):
        own_grad, other_grad = gradient_call(
            table, scored, other_half, weighed, all_stats
        )
    with jax.named_scope("exchange_out"):
        received = lax.ppermute(other_grad, ALL, swap)
        outgoing = pair_call(own_grad, received)
        back = lax.all_to_all(outgoing, ALL, split_axis=0, concat_axis=0, tiled=True)
    with jax.named_scope("sums"):
        return sums_call(back)


def solution(mesh):
    split = P(ALL, None)
    return jax.shard_map(
        shards,
        mesh=mesh,
        in_specs=(split,) * 5 + (P(),),
        out_specs=(split,) * 3,
        check_vma=False,
    )
```

```python
import jax
import jax.numpy as jnp
from jax import lax
from jax.experimental import pallas as pl
from jax.experimental.pallas import tpu as pltpu
from jax.sharding import PartitionSpec as P

ALL = ("qrow", "kcol")
DEVICES = 128
HEADS = 8
WIDTH = 128
STRETCH = 128
PLACES = 128
KEY_GROUPS = 4
ROW_GROUPS = 32
QUERY_TOKENS = 16
TOKEN_GROUPS = STRETCH // QUERY_TOKENS
PAIR = 2
HEAD_GROUPS = HEADS // PAIR
KEY_TOKENS = STRETCH // KEY_GROUPS
HALF = KEY_TOKENS // 2
ROWS = QUERY_TOKENS * PAIR
ALL_ROWS = PLACES * ROWS
ALL_KEYS = PLACES * KEY_TOKENS
TILE = 512
TILES = ALL_ROWS // TILE
SPAN = TILE // ROWS
SUBLANES = 8
SKEW = 3
HALF_TILE = TILE // 2
CHUNK = 256
NEGATIVE = -1e30
SCALE = float(WIDTH) ** (-0.5)
TO_LOG2 = SCALE * 1.4426950408889634
MIB = 1024 * 1024


def contract(left, right, left_dim, right_dim):
    return lax.dot_general(
        left, right, (((left_dim,), (right_dim,)), ((), ())), preferred_element_type=jnp.float32
    )


def tile_at(index):
    return pl.ds(pl.multiple_of(index * TILE, TILE), TILE)


def allowed_on_diagonal(key_group, row_group, row_dim):
    row = lax.broadcasted_iota(jnp.int32, (TILE, TILE), row_dim)
    column = lax.broadcasted_iota(jnp.int32, (TILE, TILE), 1 - row_dim)
    first_token = (row_group // HEAD_GROUPS) * QUERY_TOKENS
    row_place = (row // ROWS) * STRETCH + first_token + row % QUERY_TOKENS
    key_place = (column // KEY_TOKENS) * STRETCH + key_group * KEY_TOKENS + column % KEY_TOKENS
    return key_place <= row_place


def stats_kernel(table, scored, other_half, stats, query, key):
    key_group, row_group, core = table[PLACES], table[PLACES + 1], table[PLACES + 2]

    def prepare_rows(r):
        for s in range(SPAN):
            spot = slice(r * TILE + s * ROWS, r * TILE + (s + 1) * ROWS)
            scaled = scored[table[r * SPAN + s], 0:ROWS].astype(jnp.float32) * TO_LOG2
            high = scaled.astype(jnp.bfloat16)
            query[spot, 0:WIDTH] = high
            query[spot, WIDTH:] = (scaled - high.astype(jnp.float32)).astype(jnp.bfloat16)

    def prepare_keys(k):
        for s in range(SPAN):
            source = table[k * SPAN + s]
            start = k * TILE + s * KEY_TOKENS
            own_spot = pl.ds(pl.multiple_of(start + core * HALF, HALF), HALF)
            other_spot = pl.ds(pl.multiple_of(start + (1 - core) * HALF, HALF), HALF)
            own = scored[source, ROWS : ROWS + HALF]
            other = other_half[source, 0:HALF]
            key[own_spot, 0:WIDTH] = own
            key[own_spot, WIDTH:] = own
            key[other_spot, 0:WIDTH] = other
            key[other_spot, WIDTH:] = other

    allowed = allowed_on_diagonal(key_group, row_group, 1)
    state = {}

    def absorb(r, first, masked):
        scores = contract(key[first : first + CHUNK], query[r * TILE : (r + 1) * TILE], 1, 1)
        if masked:
            inside = first - r * TILE
            scores = jnp.where(allowed[inside : inside + CHUNK], scores, NEGATIVE)
        scores = scores.reshape(CHUNK // SUBLANES, SUBLANES, TILE)
        chunk_peak = jnp.max(scores, axis=0)
        if r not in state:
            raised = chunk_peak
            state[r] = raised, jnp.sum(jnp.exp2(scores - raised[None]), axis=0)
            return
        highest, summed = state[r]
        raised = jnp.maximum(highest, chunk_peak)
        summed = summed * jnp.exp2(highest - raised)
        state[r] = raised, summed + jnp.sum(jnp.exp2(scores - raised[None]), axis=0)

    def finish(r):
        highest, summed = state.pop(r)
        row_peak = jnp.max(highest, axis=0, keepdims=True)
        row_total = jnp.sum(summed * jnp.exp2(highest - row_peak), axis=0, keepdims=True)
        stats[r : r + 1] = row_peak
        stats[r + TILES : r + TILES + 1] = row_total

    for first in range(0, ALL_KEYS, CHUNK):
        if first % TILE == 0:
            prepare_keys(first // TILE)
        for r in range(first // TILE, TILES):
            if first == 0:
                prepare_rows(r)
            absorb(r, first, r == first // TILE)
        if (first + CHUNK) % TILE == 0:
            finish(first // TILE)


def gradient_kernel(
    table,
    scored,
    other_half,
    weighed,
    stats_0,
    stats_1,
    stats_2,
    stats_3,
    own_grad,
    other_grad,
    query,
    grad,
    query_turned,
    grad_turned,
    key,
    value,
    logs,
    key_sorted,
    value_sorted,
):
    key_group, row_group, core = table[PLACES], table[PLACES + 1], table[PLACES + 2]
    lane = lax.broadcasted_iota(jnp.int32, (TILE, WIDTH), 1)
    row_token = lax.broadcasted_iota(jnp.int32, (ROWS, WIDTH), 0) % QUERY_TOKENS
    row_token = row_token + (row_group // HEAD_GROUPS) * QUERY_TOKENS
    own_lane = lax.broadcasted_iota(jnp.int32, (ROWS, WIDTH), 1) == row_token
    all_stats = [ref[...] for ref in (stats_0, stats_1, stats_2, stats_3)]
    peaks = [part[0:TILES] for part in all_stats]
    highest = jnp.maximum(jnp.maximum(peaks[0], peaks[1]), jnp.maximum(peaks[2], peaks[3]))
    summed = jnp.zeros_like(highest)
    for part in all_stats:
        summed = summed + part[TILES:] * jnp.exp2(part[0:TILES] - highest)
    log_totals = (highest + jnp.log2(summed)) * (1.0 / TO_LOG2)
    high = log_totals.astype(jnp.bfloat16).astype(jnp.float32)
    middle = (log_totals - high).astype(jnp.bfloat16).astype(jnp.float32)
    low = (log_totals - high - middle).astype(jnp.bfloat16).astype(jnp.float32)
    padding = jnp.zeros((WIDTH - 3 * TILES, TILE), jnp.float32)
    logs[...] = jnp.concatenate([high, middle, low, padding], axis=0).T
    allowed = allowed_on_diagonal(key_group, row_group, 0)
    key_extra = jnp.where(lane < 3 * TILES, -1.0, 0.0).astype(jnp.bfloat16)
    value_extra = jnp.full((TILE, WIDTH), -1.0, jnp.bfloat16)

    def tile_span(t):
        return slice(t * TILE, (t + 1) * TILE)

    def prepare_rows(r):
        here = tile_span(r)
        chosen = jnp.logical_and(lane % TILES == r, lane < 3 * TILES)
        query[here, WIDTH:] = jnp.where(chosen, logs[...], 0.0).astype(jnp.bfloat16)
        for k in range(SPAN):
            source = table[r * SPAN + k]
            spot = slice(r * TILE + k * ROWS, r * TILE + (k + 1) * ROWS)
            query[spot, 0:WIDTH] = scored[source, 0:ROWS]
            grad[spot, 0:WIDTH] = weighed[source, 0:ROWS]
            delta = weighed[source, ROWS : ROWS + SUBLANES].astype(jnp.float32)
            per_row = [
                jnp.broadcast_to(delta[h : h + 1], (QUERY_TOKENS, WIDTH)) for h in range(PAIR)
            ]
            grad[spot, WIDTH:] = jnp.where(own_lane, jnp.concatenate(per_row, axis=0), 0.0).astype(
                jnp.bfloat16
            )
        query_turned[:, here] = query[here, 0:WIDTH].T
        grad_turned[:, here] = grad[here, 0:WIDTH].T

    def prepare_keys(k):
        here = tile_span(k)
        key[here, WIDTH:] = key_extra
        value[here, WIDTH:] = value_extra
        for s in range(SPAN):
            source = table[k * SPAN + s]
            start = k * TILE + s * KEY_TOKENS
            own_spot = pl.ds(pl.multiple_of(start + core * HALF, HALF), HALF)
            other_spot = pl.ds(pl.multiple_of(start + (1 - core) * HALF, HALF), HALF)
            key[own_spot, 0:WIDTH] = scored[source, ROWS : ROWS + HALF]
            key[other_spot, 0:WIDTH] = other_half[source, 0:HALF]
            value[own_spot, 0:WIDTH] = scored[source, ROWS + HALF : ROWS + 2 * HALF]
            value[other_spot, 0:WIDTH] = other_half[source, HALF : 2 * HALF]

    def first(rows_at, keys_at, masked):
        scores = contract(query[rows_at], key[keys_at], 1, 1)
        probs = jnp.exp2(scores * TO_LOG2)
        if masked:
            probs = jnp.where(allowed[: scores.shape[0], : scores.shape[1]], probs, 0.0)
        moved_probs = contract(grad[rows_at], value[keys_at], 1, 1)
        return probs.astype(jnp.bfloat16), (probs * moved_probs).astype(jnp.bfloat16)

    value_sums, key_sums, query_sums = {}, {}, {}

    def add(sums, spot, part):
        sums[spot] = sums[spot] + part if spot in sums else part

    def second(r, k, rows_at, keys_at, probs_low, dscores):
        value_part = contract(grad_turned[:, rows_at], probs_low, 1, 0)
        key_part = contract(query_turned[:, rows_at], dscores, 1, 0)
        query_part = contract(dscores, key[keys_at, 0:WIDTH], 1, 0)
        row_start = rows_at.start - r * TILE
        key_start = keys_at.start - k * TILE
        for n in range((rows_at.stop - rows_at.start) // HALF_TILE):
            span = slice(n * HALF_TILE, (n + 1) * HALF_TILE)
            add(query_sums, (r, row_start // HALF_TILE + n), query_part[span])
        for n in range((keys_at.stop - keys_at.start) // HALF_TILE):
            span = slice(n * HALF_TILE, (n + 1) * HALF_TILE)
            add(value_sums, (k, key_start // HALF_TILE + n), value_part[:, span])
            add(key_sums, (k, key_start // HALF_TILE + n), key_part[:, span])

    def finish_rows(r):
        for n in range(2):
            total = (query_sums.pop((r, n)) * SCALE).astype(jnp.bfloat16)
            for s in range(SPAN // 2):
                source = table[r * SPAN + n * SPAN // 2 + s]
                own_grad[source, 0:ROWS] = total[s * ROWS : (s + 1) * ROWS]

    def finish_keys(k):
        for n in range(2):
            here = slice(k * TILE + n * HALF_TILE, k * TILE + (n + 1) * HALF_TILE)
            key_sorted[here] = (key_sums.pop((k, n)) * SCALE).astype(jnp.bfloat16).T
            value_sorted[here] = value_sums.pop((k, n)).astype(jnp.bfloat16).T

    def blocks():
        for k in range(TILES):
            middle = k * TILE + HALF_TILE
            late = slice(middle, (k + 1) * TILE)
            yield k, k, tile_span(k), slice(k * TILE, middle), True
            yield k, k, late, late, True
            for r in range(k + 1, TILES):
                yield r, k, tile_span(r), tile_span(k), False

    left = {}
    for r, k, *_ in blocks():
        left["rows", r] = left.get(("rows", r), 0) + 1
        left["keys", k] = left.get(("keys", k), 0) + 1

    def retire(r, k, *rest):
        second(r, k, *rest)
        left["rows", r] -= 1
        left["keys", k] -= 1
        if left["rows", r] == 0:
            finish_rows(r)
        if left["keys", k] == 0:
            finish_keys(k)

    waiting = []
    ready = set()
    for r, k, rows_at, keys_at, masked in blocks():
        if k not in ready:
            ready.add(k)
            prepare_keys(k)
        if k == 0 and ("rows", r) not in ready:
            ready.add(("rows", r))
            prepare_rows(r)
        waiting.append((r, k, rows_at, keys_at) + first(rows_at, keys_at, masked))
        if len(waiting) > SKEW:
            retire(*waiting.pop(0))
    for entry in waiting:
        retire(*entry)

    def unsort(place, carry):
        source = table[place]
        first = pl.ds(pl.multiple_of(place * KEY_TOKENS + core * HALF, HALF), HALF)
        second = pl.ds(pl.multiple_of(place * KEY_TOKENS + (1 - core) * HALF, HALF), HALF)
        own_grad[source, ROWS : ROWS + HALF] = key_sorted[first]
        own_grad[source, ROWS + HALF :] = value_sorted[first]
        other_grad[source, 0:HALF] = key_sorted[second]
        other_grad[source, HALF:] = value_sorted[second]
        return carry

    lax.fori_loop(0, PLACES, unsort, 0, unroll=8)


IN_VMEM = pl.BlockSpec(memory_space=pltpu.VMEM)
IN_SMEM = pl.BlockSpec(memory_space=pltpu.SMEM)
PAIRS = TILE * TILE * TILES * (TILES + 1) // 2


def stats_call(table, scored, other_half):
    return pl.pallas_call(
        stats_kernel,
        out_shape=jax.ShapeDtypeStruct((2 * TILES, TILE), jnp.float32),
        in_specs=[IN_SMEM, IN_VMEM, IN_VMEM],
        out_specs=IN_VMEM,
        scratch_shapes=[
            pltpu.VMEM((ALL_ROWS, 2 * WIDTH), jnp.bfloat16),
            pltpu.VMEM((ALL_KEYS, 2 * WIDTH), jnp.bfloat16),
        ],
        compiler_params=pltpu.CompilerParams(vmem_limit_bytes=20 * MIB),
        cost_estimate=pl.CostEstimate(
            flops=2 * PAIRS * WIDTH, bytes_accessed=4 * MIB, transcendentals=PAIRS
        ),
        name="softmax_totals",
    )(table, scored, other_half)


def gradient_call(table, scored, other_half, weighed, stats):
    own = jax.ShapeDtypeStruct((PLACES, ROWS + 2 * HALF, WIDTH), jnp.bfloat16)
    other = jax.ShapeDtypeStruct((PLACES, 2 * HALF, WIDTH), jnp.bfloat16)
    return pl.pallas_call(
        gradient_kernel,
        out_shape=(own, other),
        in_specs=[IN_SMEM] + [IN_VMEM] * 7,
        out_specs=(IN_VMEM,) * 2,
        scratch_shapes=[
            pltpu.VMEM((ALL_ROWS, 2 * WIDTH), jnp.bfloat16),
            pltpu.VMEM((ALL_ROWS, 2 * WIDTH), jnp.bfloat16),
            pltpu.VMEM((WIDTH, ALL_ROWS), jnp.bfloat16),
            pltpu.VMEM((WIDTH, ALL_ROWS), jnp.bfloat16),
            pltpu.VMEM((ALL_KEYS, 2 * WIDTH), jnp.bfloat16),
            pltpu.VMEM((ALL_KEYS, 2 * WIDTH), jnp.bfloat16),
            pltpu.VMEM((TILE, WIDTH), jnp.float32),
            pltpu.VMEM((ALL_KEYS, WIDTH), jnp.bfloat16),
            pltpu.VMEM((ALL_KEYS, WIDTH), jnp.bfloat16),
        ],
        compiler_params=pltpu.CompilerParams(vmem_limit_bytes=32 * MIB),
        cost_estimate=pl.CostEstimate(
            flops=10 * PAIRS * WIDTH, bytes_accessed=8 * MIB, transcendentals=PAIRS
        ),
        name="gradients",
    )(table, scored, other_half, weighed, *stats)


def pack_rows(rows, outgoing):
    for r in range(ROW_GROUPS):
        tokens = (r // HEAD_GROUPS) * QUERY_TOKENS
        for h in range(PAIR):
            head = (r % HEAD_GROUPS) * PAIR + h
            part = rows[tokens : tokens + QUERY_TOKENS, head * WIDTH : (head + 1) * WIDTH]
            for g in range(KEY_GROUPS):
                outgoing[
                    g * ROW_GROUPS + r, h * QUERY_TOKENS : (h + 1) * QUERY_TOKENS
                ] = part


def pack_kernel(rows, keys, values, outgoing):
    pack_rows(rows, outgoing)
    for g in range(KEY_GROUPS):
        for c in range(2):
            first = g * KEY_TOKENS + c * HALF
            for n, array in enumerate((keys, values)):
                part = array[first : first + HALF]
                spot = slice(ROWS + n * HALF, ROWS + (n + 1) * HALF)
                for r in range(c, ROW_GROUPS, 2):
                    outgoing[g * ROW_GROUPS + r, spot] = part


def pack_grad_kernel(rows, forward, outgoing):
    pack_rows(rows, outgoing)
    lane = lax.broadcasted_iota(jnp.int32, (STRETCH, WIDTH), 1)
    delta = jnp.zeros((STRETCH, WIDTH), jnp.float32)
    for head in range(HEADS):
        span = slice(head * WIDTH, (head + 1) * WIDTH)
        products = rows[:, span].astype(jnp.float32) * forward[:, span].astype(jnp.float32)
        delta = jnp.where(lane == head, jnp.sum(products, axis=1, keepdims=True), delta)
    delta = delta.T
    blank = jnp.zeros((SUBLANES - PAIR, WIDTH), jnp.float32)
    for p in range(HEAD_GROUPS):
        part = jnp.concatenate([delta[PAIR * p : PAIR * (p + 1)], blank], axis=0)
        part = part.astype(jnp.bfloat16)
        for r in range(p, DEVICES, HEAD_GROUPS):
            outgoing[r, ROWS : ROWS + SUBLANES] = part


def pack_call(kernel, height, *arrays):
    return pl.pallas_call(
        kernel,
        out_shape=jax.ShapeDtypeStruct((DEVICES, height, WIDTH), jnp.bfloat16),
        in_specs=[IN_VMEM] * len(arrays),
        out_specs=IN_VMEM,
        compiler_params=pltpu.CompilerParams(vmem_limit_bytes=56 * MIB),
        name="pack",
    )(*arrays)


def pair_kernel(own, received, outgoing):
    outgoing[:, 0:ROWS] = own[:, 0:ROWS]
    total = own[:, ROWS:].astype(jnp.float32) + received[...].astype(jnp.float32)
    outgoing[:, ROWS:] = total.astype(jnp.bfloat16)


def pair_call(own, received):
    return pl.pallas_call(
        pair_kernel,
        out_shape=jax.ShapeDtypeStruct(own.shape, own.dtype),
        in_specs=[IN_VMEM] * 2,
        out_specs=IN_VMEM,
        compiler_params=pltpu.CompilerParams(vmem_limit_bytes=16 * MIB),
        name="pair_sum",
    )(own, received)


def sums_kernel(back, d_query, d_key, d_value):
    for r in range(ROW_GROUPS):
        total = back[r, 0:ROWS].astype(jnp.float32)
        for g in range(1, KEY_GROUPS):
            total = total + back[g * ROW_GROUPS + r, 0:ROWS].astype(jnp.float32)
        total = total.astype(jnp.bfloat16)
        tokens = (r // HEAD_GROUPS) * QUERY_TOKENS
        for h in range(PAIR):
            head = (r % HEAD_GROUPS) * PAIR + h
            d_query[tokens : tokens + QUERY_TOKENS, head * WIDTH : (head + 1) * WIDTH] = total[
                h * QUERY_TOKENS : (h + 1) * QUERY_TOKENS
            ]
    for g in range(KEY_GROUPS):
        for c in range(2):
            total = jnp.zeros((2 * HALF, WIDTH), jnp.float32)
            for r in range(c, ROW_GROUPS, 2):
                total = total + back[g * ROW_GROUPS + r, ROWS:].astype(jnp.float32)
            first = g * KEY_TOKENS + c * HALF
            d_key[first : first + HALF] = total[0:HALF].astype(jnp.bfloat16)
            d_value[first : first + HALF] = total[HALF:].astype(jnp.bfloat16)


def sums_call(back):
    small = jax.ShapeDtypeStruct((STRETCH, WIDTH), jnp.bfloat16)
    return pl.pallas_call(
        sums_kernel,
        out_shape=(
            jax.ShapeDtypeStruct((STRETCH, HEADS * WIDTH), jnp.bfloat16),
            small,
            small,
        ),
        in_specs=[IN_VMEM],
        out_specs=(IN_VMEM,) * 3,
        compiler_params=pltpu.CompilerParams(vmem_limit_bytes=12 * MIB),
        name="sums",
    )(back)


def shards(queries, key_states, value_states, out_grad, forward_out, stretch_order):
    me = lax.axis_index(ALL)
    swap = [(d, d ^ 1) for d in range(DEVICES)]

    def around(step):
        return [(d, (d + step * ROW_GROUPS) % DEVICES) for d in range(DEVICES)]

    with jax.named_scope("outgoing"):
        scored = pack_call(pack_kernel, ROWS + 2 * HALF, queries, key_states, value_states)
        weighed = pack_call(pack_grad_kernel, ROWS + SUBLANES, out_grad, forward_out)
    with jax.named_scope("table"):
        places = jnp.arange(PLACES, dtype=jnp.int32)
        holder = jnp.sum(
            jnp.where(stretch_order[None, :] == places[:, None], places[None, :], 0), axis=1
        )
        ids = jnp.stack([me // ROW_GROUPS, me % ROW_GROUPS, me % 2]).astype(jnp.int32)
        table = jnp.concatenate([holder, ids])
    with jax.named_scope("exchange_in"):
        scored = lax.all_to_all(scored, ALL, split_axis=0, concat_axis=0, tiled=True)
        scored, weighed = lax.optimization_barrier((scored, weighed))
        weighed = lax.all_to_all(weighed, ALL, split_axis=0, concat_axis=0, tiled=True)
        other_half = lax.ppermute(scored[:, ROWS:], ALL, swap)
    with jax.named_scope("totals"):
        stats = stats_call(table, scored, other_half)
        all_stats = [stats] + [lax.ppermute(stats, ALL, around(k)) for k in range(1, KEY_GROUPS)]
        weighed, all_stats = lax.optimization_barrier((weighed, all_stats))
    with jax.named_scope("gradients"):
        own_grad, other_grad = gradient_call(
            table, scored, other_half, weighed, all_stats
        )
    with jax.named_scope("exchange_out"):
        received = lax.ppermute(other_grad, ALL, swap)
        outgoing = pair_call(own_grad, received)
        back = lax.all_to_all(outgoing, ALL, split_axis=0, concat_axis=0, tiled=True)
    with jax.named_scope("sums"):
        return sums_call(back)


def solution(mesh):
    split = P(ALL, None)
    return jax.shard_map(
        shards,
        mesh=mesh,
        in_specs=(split,) * 5 + (P(),),
        out_specs=(split,) * 3,
        check_vma=False,
    )
```

```python
import jax
import jax.numpy as jnp
from jax import lax
from jax.experimental import pallas as pl
from jax.experimental.pallas import tpu as pltpu
from jax.sharding import PartitionSpec as P

ALL = ("qrow", "kcol")
DEVICES = 128
HEADS = 8
WIDTH = 128
STRETCH = 128
PLACES = 128
KEY_GROUPS = 4
ROW_GROUPS = 32
QUERY_TOKENS = 16
TOKEN_GROUPS = STRETCH // QUERY_TOKENS
PAIR = 2
HEAD_GROUPS = HEADS // PAIR
KEY_TOKENS = STRETCH // KEY_GROUPS
HALF = KEY_TOKENS // 2
ROWS = QUERY_TOKENS * PAIR
ALL_ROWS = PLACES * ROWS
ALL_KEYS = PLACES * KEY_TOKENS
TILE = 512
TILES = ALL_ROWS // TILE
SPAN = TILE // ROWS
SUBLANES = 8
SKEW = 3
HALF_TILE = TILE // 2
CHUNK = 256
NEGATIVE = -1e30
SCALE = float(WIDTH) ** (-0.5)
TO_LOG2 = SCALE * 1.4426950408889634
MIB = 1024 * 1024


def contract(left, right, left_dim, right_dim):
    return lax.dot_general(
        left, right, (((left_dim,), (right_dim,)), ((), ())), preferred_element_type=jnp.float32
    )


def tile_at(index):
    return pl.ds(pl.multiple_of(index * TILE, TILE), TILE)


def allowed_on_diagonal(key_group, row_group, row_dim):
    row = lax.broadcasted_iota(jnp.int32, (TILE, TILE), row_dim)
    column = lax.broadcasted_iota(jnp.int32, (TILE, TILE), 1 - row_dim)
    first_token = (row_group // HEAD_GROUPS) * QUERY_TOKENS
    row_place = (row // ROWS) * STRETCH + first_token + row % QUERY_TOKENS
    key_place = (column // KEY_TOKENS) * STRETCH + key_group * KEY_TOKENS + column % KEY_TOKENS
    return key_place <= row_place


def stats_kernel(table, scored, other_half, stats, query, key):
    key_group, row_group, core = table[PLACES], table[PLACES + 1], table[PLACES + 2]

    def prepare_rows(r):
        for s in range(SPAN):
            spot = slice(r * TILE + s * ROWS, r * TILE + (s + 1) * ROWS)
            scaled = scored[table[r * SPAN + s], 0:ROWS].astype(jnp.float32) * TO_LOG2
            high = scaled.astype(jnp.bfloat16)
            query[spot, 0:WIDTH] = high
            query[spot, WIDTH:] = (scaled - high.astype(jnp.float32)).astype(jnp.bfloat16)

    def prepare_keys(k):
        for s in range(SPAN):
            source = table[k * SPAN + s]
            start = k * TILE + s * KEY_TOKENS
            own_spot = pl.ds(pl.multiple_of(start + core * HALF, HALF), HALF)
            other_spot = pl.ds(pl.multiple_of(start + (1 - core) * HALF, HALF), HALF)
            own = scored[source, ROWS : ROWS + HALF]
            other = other_half[source, ROWS : ROWS + HALF]
            key[own_spot, 0:WIDTH] = own
            key[own_spot, WIDTH:] = own
            key[other_spot, 0:WIDTH] = other
            key[other_spot, WIDTH:] = other

    allowed = allowed_on_diagonal(key_group, row_group, 1)
    state = {}

    def absorb(r, first, masked):
        begin = HALF_TILE if masked and first % TILE >= HALF_TILE else 0
        rows = slice(r * TILE + begin, (r + 1) * TILE)
        scores = contract(key[first : first + CHUNK], query[rows], 1, 1)
        if masked:
            inside = first - r * TILE
            scores = jnp.where(allowed[inside : inside + CHUNK, begin:], scores, NEGATIVE)
        scores = scores.reshape(CHUNK // SUBLANES, SUBLANES, TILE - begin)
        for n in range(begin // HALF_TILE, 2):
            part = scores[..., n * HALF_TILE - begin : (n + 1) * HALF_TILE - begin]
            raised = jnp.max(part, axis=0)
            if (r, n) in state:
                highest, summed = state[r, n]
                raised = jnp.maximum(highest, raised)
                summed = summed * jnp.exp2(highest - raised)
                summed = summed + jnp.sum(jnp.exp2(part - raised[None]), axis=0)
            else:
                summed = jnp.sum(jnp.exp2(part - raised[None]), axis=0)
            state[r, n] = raised, summed

    def finish(r):
        for n in range(2):
            highest, summed = state.pop((r, n))
            row_peak = jnp.max(highest, axis=0, keepdims=True)
            row_total = jnp.sum(summed * jnp.exp2(highest - row_peak), axis=0, keepdims=True)
            lanes = slice(n * HALF_TILE, (n + 1) * HALF_TILE)
            stats[r : r + 1, lanes] = row_peak
            stats[r + TILES : r + TILES + 1, lanes] = row_total

    for first in range(0, ALL_KEYS, CHUNK):
        if first % TILE == 0:
            prepare_keys(first // TILE)
        for r in range(first // TILE, TILES):
            if first == 0:
                prepare_rows(r)
            absorb(r, first, r == first // TILE)
        if (first + CHUNK) % TILE == 0:
            finish(first // TILE)


def gradient_kernel(
    table,
    scored,
    other_half,
    weighed,
    stats_0,
    stats_1,
    stats_2,
    stats_3,
    own_grad,
    other_grad,
    query,
    grad,
    query_turned,
    grad_turned,
    key,
    value,
    logs,
    key_sorted,
    value_sorted,
):
    key_group, row_group, core = table[PLACES], table[PLACES + 1], table[PLACES + 2]
    lane = lax.broadcasted_iota(jnp.int32, (TILE, WIDTH), 1)
    row_token = lax.broadcasted_iota(jnp.int32, (ROWS, WIDTH), 0) % QUERY_TOKENS
    row_token = row_token + (row_group // HEAD_GROUPS) * QUERY_TOKENS
    own_lane = lax.broadcasted_iota(jnp.int32, (ROWS, WIDTH), 1) == row_token
    all_stats = [ref[...] for ref in (stats_0, stats_1, stats_2, stats_3)]
    peaks = [part[0:TILES] for part in all_stats]
    highest = jnp.maximum(jnp.maximum(peaks[0], peaks[1]), jnp.maximum(peaks[2], peaks[3]))
    summed = jnp.zeros_like(highest)
    for part in all_stats:
        summed = summed + part[TILES:] * jnp.exp2(part[0:TILES] - highest)
    log_totals = (highest + jnp.log2(summed)) * (1.0 / TO_LOG2)
    high = log_totals.astype(jnp.bfloat16).astype(jnp.float32)
    middle = (log_totals - high).astype(jnp.bfloat16).astype(jnp.float32)
    low = (log_totals - high - middle).astype(jnp.bfloat16).astype(jnp.float32)
    padding = jnp.zeros((WIDTH - 3 * TILES, TILE), jnp.float32)
    logs[...] = jnp.concatenate([high, middle, low, padding], axis=0).T
    allowed = allowed_on_diagonal(key_group, row_group, 0)
    key_extra = jnp.where(lane < 3 * TILES, -1.0, 0.0).astype(jnp.bfloat16)
    value_extra = jnp.full((TILE, WIDTH), -1.0, jnp.bfloat16)

    def tile_span(t):
        return slice(t * TILE, (t + 1) * TILE)

    def prepare_rows(r):
        here = tile_span(r)
        chosen = jnp.logical_and(lane % TILES == r, lane < 3 * TILES)
        query[here, WIDTH:] = jnp.where(chosen, logs[...], 0.0).astype(jnp.bfloat16)
        for k in range(SPAN):
            source = table[r * SPAN + k]
            spot = slice(r * TILE + k * ROWS, r * TILE + (k + 1) * ROWS)
            query[spot, 0:WIDTH] = scored[source, 0:ROWS]
            grad[spot, 0:WIDTH] = weighed[source, 0:ROWS]
            delta = weighed[source, ROWS : ROWS + SUBLANES].astype(jnp.float32)
            per_row = [
                jnp.broadcast_to(delta[h : h + 1], (QUERY_TOKENS, WIDTH)) for h in range(PAIR)
            ]
            grad[spot, WIDTH:] = jnp.where(own_lane, jnp.concatenate(per_row, axis=0), 0.0).astype(
                jnp.bfloat16
            )
        query_turned[:, here] = query[here, 0:WIDTH].T
        grad_turned[:, here] = grad[here, 0:WIDTH].T

    def prepare_keys(k):
        here = tile_span(k)
        key[here, WIDTH:] = key_extra
        value[here, WIDTH:] = value_extra
        for s in range(SPAN):
            source = table[k * SPAN + s]
            start = k * TILE + s * KEY_TOKENS
            own_spot = pl.ds(pl.multiple_of(start + core * HALF, HALF), HALF)
            other_spot = pl.ds(pl.multiple_of(start + (1 - core) * HALF, HALF), HALF)
            key[own_spot, 0:WIDTH] = scored[source, ROWS : ROWS + HALF]
            key[other_spot, 0:WIDTH] = other_half[source, ROWS : ROWS + HALF]
            value[own_spot, 0:WIDTH] = scored[source, ROWS + HALF : ROWS + 2 * HALF]
            value[other_spot, 0:WIDTH] = other_half[source, ROWS + HALF :]

    def first(rows_at, keys_at, masked):
        scores = contract(query[rows_at], key[keys_at], 1, 1)
        probs = jnp.exp2(scores * TO_LOG2)
        if masked:
            probs = jnp.where(allowed[: scores.shape[0], : scores.shape[1]], probs, 0.0)
        moved_probs = contract(grad[rows_at], value[keys_at], 1, 1)
        return probs.astype(jnp.bfloat16), (probs * moved_probs).astype(jnp.bfloat16)

    value_sums, key_sums, query_sums = {}, {}, {}

    def add(sums, spot, part):
        sums[spot] = sums[spot] + part if spot in sums else part

    def second(r, k, rows_at, keys_at, probs_low, dscores):
        value_part = contract(grad_turned[:, rows_at], probs_low, 1, 0)
        key_part = contract(query_turned[:, rows_at], dscores, 1, 0)
        query_part = contract(dscores, key[keys_at, 0:WIDTH], 1, 0)
        row_start = rows_at.start - r * TILE
        key_start = keys_at.start - k * TILE
        for n in range((rows_at.stop - rows_at.start) // HALF_TILE):
            span = slice(n * HALF_TILE, (n + 1) * HALF_TILE)
            add(query_sums, (r, row_start // HALF_TILE + n), query_part[span])
        for n in range((keys_at.stop - keys_at.start) // HALF_TILE):
            span = slice(n * HALF_TILE, (n + 1) * HALF_TILE)
            add(value_sums, (k, key_start // HALF_TILE + n), value_part[:, span])
            add(key_sums, (k, key_start // HALF_TILE + n), key_part[:, span])

    def finish_rows(r):
        for n in range(2):
            total = (query_sums.pop((r, n)) * SCALE).astype(jnp.bfloat16)
            for s in range(SPAN // 2):
                source = table[r * SPAN + n * SPAN // 2 + s]
                own_grad[source, 0:ROWS] = total[s * ROWS : (s + 1) * ROWS]

    def finish_keys(k):
        for n in range(2):
            here = slice(k * TILE + n * HALF_TILE, k * TILE + (n + 1) * HALF_TILE)
            key_sorted[here] = (key_sums.pop((k, n)) * SCALE).astype(jnp.bfloat16).T
            value_sorted[here] = value_sums.pop((k, n)).astype(jnp.bfloat16).T
            for s in range(n * SPAN // 2, (n + 1) * SPAN // 2):
                source = table[k * SPAN + s]
                start = k * TILE + s * KEY_TOKENS
                own_spot = pl.ds(pl.multiple_of(start + core * HALF, HALF), HALF)
                other_spot = pl.ds(pl.multiple_of(start + (1 - core) * HALF, HALF), HALF)
                own_grad[source, ROWS : ROWS + HALF] = key_sorted[own_spot]
                own_grad[source, ROWS + HALF :] = value_sorted[own_spot]
                other_grad[source, 0:HALF] = key_sorted[other_spot]
                other_grad[source, HALF:] = value_sorted[other_spot]

    def blocks():
        for k in range(TILES):
            middle = k * TILE + HALF_TILE
            late = slice(middle, (k + 1) * TILE)
            yield k, k, tile_span(k), slice(k * TILE, middle), True
            yield k, k, late, late, True
            for r in range(k + 1, TILES):
                yield r, k, tile_span(r), tile_span(k), False

    left = {}
    for r, k, *_ in blocks():
        left["rows", r] = left.get(("rows", r), 0) + 1
        left["keys", k] = left.get(("keys", k), 0) + 1

    def retire(r, k, *rest):
        second(r, k, *rest)
        left["rows", r] -= 1
        left["keys", k] -= 1
        if left["rows", r] == 0:
            finish_rows(r)
        if left["keys", k] == 0:
            finish_keys(k)

    waiting = []
    ready = set()
    for r, k, rows_at, keys_at, masked in blocks():
        if k not in ready:
            ready.add(k)
            prepare_keys(k)
        if k == 0 and ("rows", r) not in ready:
            ready.add(("rows", r))
            prepare_rows(r)
        waiting.append((r, k, rows_at, keys_at) + first(rows_at, keys_at, masked))
        if len(waiting) > SKEW:
            retire(*waiting.pop(0))
    for entry in waiting:
        retire(*entry)


IN_VMEM = pl.BlockSpec(memory_space=pltpu.VMEM)
IN_SMEM = pl.BlockSpec(memory_space=pltpu.SMEM)
PAIRS = TILE * TILE * TILES * (TILES + 1) // 2


def stats_call(table, scored, other_half):
    return pl.pallas_call(
        stats_kernel,
        out_shape=jax.ShapeDtypeStruct((2 * TILES, TILE), jnp.float32),
        in_specs=[IN_SMEM, IN_VMEM, IN_VMEM],
        out_specs=IN_VMEM,
        scratch_shapes=[
            pltpu.VMEM((ALL_ROWS, 2 * WIDTH), jnp.bfloat16),
            pltpu.VMEM((ALL_KEYS, 2 * WIDTH), jnp.bfloat16),
        ],
        compiler_params=pltpu.CompilerParams(vmem_limit_bytes=20 * MIB),
        cost_estimate=pl.CostEstimate(
            flops=2 * PAIRS * WIDTH, bytes_accessed=4 * MIB, transcendentals=PAIRS
        ),
        name="softmax_totals",
    )(table, scored, other_half)


def gradient_call(table, scored, other_half, weighed, stats):
    own = jax.ShapeDtypeStruct((PLACES, ROWS + 2 * HALF, WIDTH), jnp.bfloat16)
    other = jax.ShapeDtypeStruct((PLACES, 2 * HALF, WIDTH), jnp.bfloat16)
    return pl.pallas_call(
        gradient_kernel,
        out_shape=(own, other),
        in_specs=[IN_SMEM] + [IN_VMEM] * 7,
        out_specs=(IN_VMEM,) * 2,
        scratch_shapes=[
            pltpu.VMEM((ALL_ROWS, 2 * WIDTH), jnp.bfloat16),
            pltpu.VMEM((ALL_ROWS, 2 * WIDTH), jnp.bfloat16),
            pltpu.VMEM((WIDTH, ALL_ROWS), jnp.bfloat16),
            pltpu.VMEM((WIDTH, ALL_ROWS), jnp.bfloat16),
            pltpu.VMEM((ALL_KEYS, 2 * WIDTH), jnp.bfloat16),
            pltpu.VMEM((ALL_KEYS, 2 * WIDTH), jnp.bfloat16),
            pltpu.VMEM((TILE, WIDTH), jnp.float32),
            pltpu.VMEM((ALL_KEYS, WIDTH), jnp.bfloat16),
            pltpu.VMEM((ALL_KEYS, WIDTH), jnp.bfloat16),
        ],
        compiler_params=pltpu.CompilerParams(vmem_limit_bytes=32 * MIB),
        cost_estimate=pl.CostEstimate(
            flops=10 * PAIRS * WIDTH, bytes_accessed=8 * MIB, transcendentals=PAIRS
        ),
        name="gradients",
    )(table, scored, other_half, weighed, *stats)


def pack_rows(rows, outgoing):
    for r in range(ROW_GROUPS):
        tokens = (r // HEAD_GROUPS) * QUERY_TOKENS
        for h in range(PAIR):
            head = (r % HEAD_GROUPS) * PAIR + h
            part = rows[tokens : tokens + QUERY_TOKENS, head * WIDTH : (head + 1) * WIDTH]
            for g in range(KEY_GROUPS):
                outgoing[
                    g * ROW_GROUPS + r, h * QUERY_TOKENS : (h + 1) * QUERY_TOKENS
                ] = part


def pack_kernel(rows, keys, values, outgoing):
    pack_rows(rows, outgoing)
    for g in range(KEY_GROUPS):
        for c in range(2):
            first = g * KEY_TOKENS + c * HALF
            for n, array in enumerate((keys, values)):
                part = array[first : first + HALF]
                spot = slice(ROWS + n * HALF, ROWS + (n + 1) * HALF)
                for r in range(c, ROW_GROUPS, 2):
                    outgoing[g * ROW_GROUPS + r, spot] = part


def pack_grad_kernel(rows, forward, outgoing):
    pack_rows(rows, outgoing)
    lane = lax.broadcasted_iota(jnp.int32, (STRETCH, WIDTH), 1)
    delta = jnp.zeros((STRETCH, WIDTH), jnp.float32)
    for head in range(HEADS):
        span = slice(head * WIDTH, (head + 1) * WIDTH)
        products = rows[:, span].astype(jnp.float32) * forward[:, span].astype(jnp.float32)
        delta = jnp.where(lane == head, jnp.sum(products, axis=1, keepdims=True), delta)
    delta = delta.T
    blank = jnp.zeros((SUBLANES - PAIR, WIDTH), jnp.float32)
    for p in range(HEAD_GROUPS):
        part = jnp.concatenate([delta[PAIR * p : PAIR * (p + 1)], blank], axis=0)
        part = part.astype(jnp.bfloat16)
        for r in range(p, DEVICES, HEAD_GROUPS):
            outgoing[r, ROWS : ROWS + SUBLANES] = part


def pack_call(kernel, height, *arrays):
    return pl.pallas_call(
        kernel,
        out_shape=jax.ShapeDtypeStruct((DEVICES, height, WIDTH), jnp.bfloat16),
        in_specs=[IN_VMEM] * len(arrays),
        out_specs=IN_VMEM,
        compiler_params=pltpu.CompilerParams(vmem_limit_bytes=56 * MIB),
        name="pack",
    )(*arrays)


def pair_kernel(own, received, outgoing):
    outgoing[:, 0:ROWS] = own[:, 0:ROWS]
    total = own[:, ROWS:].astype(jnp.float32) + received[...].astype(jnp.float32)
    outgoing[:, ROWS:] = total.astype(jnp.bfloat16)


def pair_call(own, received):
    return pl.pallas_call(
        pair_kernel,
        out_shape=jax.ShapeDtypeStruct(own.shape, own.dtype),
        in_specs=[IN_VMEM] * 2,
        out_specs=IN_VMEM,
        compiler_params=pltpu.CompilerParams(vmem_limit_bytes=16 * MIB),
        name="pair_sum",
    )(own, received)


def sums_kernel(back, d_query, d_key, d_value):
    for r in range(ROW_GROUPS):
        total = back[r, 0:ROWS].astype(jnp.float32)
        for g in range(1, KEY_GROUPS):
            total = total + back[g * ROW_GROUPS + r, 0:ROWS].astype(jnp.float32)
        total = total.astype(jnp.bfloat16)
        tokens = (r // HEAD_GROUPS) * QUERY_TOKENS
        for h in range(PAIR):
            head = (r % HEAD_GROUPS) * PAIR + h
            d_query[tokens : tokens + QUERY_TOKENS, head * WIDTH : (head + 1) * WIDTH] = total[
                h * QUERY_TOKENS : (h + 1) * QUERY_TOKENS
            ]
    for g in range(KEY_GROUPS):
        for c in range(2):
            total = jnp.zeros((2 * HALF, WIDTH), jnp.float32)
            for r in range(c, ROW_GROUPS, 2):
                total = total + back[g * ROW_GROUPS + r, ROWS:].astype(jnp.float32)
            first = g * KEY_TOKENS + c * HALF
            d_key[first : first + HALF] = total[0:HALF].astype(jnp.bfloat16)
            d_value[first : first + HALF] = total[HALF:].astype(jnp.bfloat16)


def sums_call(back):
    small = jax.ShapeDtypeStruct((STRETCH, WIDTH), jnp.bfloat16)
    return pl.pallas_call(
        sums_kernel,
        out_shape=(
            jax.ShapeDtypeStruct((STRETCH, HEADS * WIDTH), jnp.bfloat16),
            small,
            small,
        ),
        in_specs=[IN_VMEM],
        out_specs=(IN_VMEM,) * 3,
        compiler_params=pltpu.CompilerParams(vmem_limit_bytes=12 * MIB),
        name="sums",
    )(back)


def shards(queries, key_states, value_states, out_grad, forward_out, stretch_order):
    me = lax.axis_index(ALL)
    swap = [(d, d ^ 1) for d in range(DEVICES)]

    def around(step):
        return [(d, (d + step * ROW_GROUPS) % DEVICES) for d in range(DEVICES)]

    with jax.named_scope("outgoing"):
        scored = pack_call(pack_kernel, ROWS + 2 * HALF, queries, key_states, value_states)
        weighed = pack_call(pack_grad_kernel, ROWS + SUBLANES, out_grad, forward_out)
    with jax.named_scope("table"):
        places = jnp.arange(PLACES, dtype=jnp.int32)
        holder = jnp.sum(
            jnp.where(stretch_order[None, :] == places[:, None], places[None, :], 0), axis=1
        )
        ids = jnp.stack([me // ROW_GROUPS, me % ROW_GROUPS, me % 2]).astype(jnp.int32)
        table = jnp.concatenate([holder, ids])
    with jax.named_scope("exchange_in"):
        scored = lax.all_to_all(scored, ALL, split_axis=0, concat_axis=0, tiled=True)
        scored, weighed = lax.optimization_barrier((scored, weighed))
        weighed = lax.all_to_all(weighed, ALL, split_axis=0, concat_axis=0, tiled=True)
        other_half = lax.ppermute(scored, ALL, swap)
    with jax.named_scope("totals"):
        stats = stats_call(table, scored, other_half)
        all_stats = [stats] + [lax.ppermute(stats, ALL, around(k)) for k in range(1, KEY_GROUPS)]
        weighed, all_stats = lax.optimization_barrier((weighed, all_stats))
    with jax.named_scope("gradients"):
        own_grad, other_grad = gradient_call(
            table, scored, other_half, weighed, all_stats
        )
    with jax.named_scope("exchange_out"):
        received = lax.ppermute(other_grad, ALL, swap)
        outgoing = pair_call(own_grad, received)
        back = lax.all_to_all(outgoing, ALL, split_axis=0, concat_axis=0, tiled=True)
    with jax.named_scope("sums"):
        return sums_call(back)


def solution(mesh):
    split = P(ALL, None)
    return jax.shard_map(
        shards,
        mesh=mesh,
        in_specs=(split,) * 5 + (P(),),
        out_specs=(split,) * 3,
        check_vma=False,
    )
```

```python
import jax
import jax.numpy as jnp
from jax import lax
from jax.experimental import pallas as pl
from jax.experimental.pallas import tpu as pltpu
from jax.sharding import PartitionSpec as P

ALL = ("qrow", "kcol")
DEVICES = 128
HEADS = 8
WIDTH = 128
STRETCH = 128
PLACES = 128
KEY_GROUPS = 4
ROW_GROUPS = 32
QUERY_TOKENS = 16
TOKEN_GROUPS = STRETCH // QUERY_TOKENS
PAIR = 2
HEAD_GROUPS = HEADS // PAIR
KEY_TOKENS = STRETCH // KEY_GROUPS
HALF = KEY_TOKENS // 2
ROWS = QUERY_TOKENS * PAIR
ALL_ROWS = PLACES * ROWS
ALL_KEYS = PLACES * KEY_TOKENS
TILE = 512
TILES = ALL_ROWS // TILE
SPAN = TILE // ROWS
SUBLANES = 8
SKEW = 3
HALF_TILE = TILE // 2
CHUNK = 256
NEGATIVE = -1e30
SCALE = float(WIDTH) ** (-0.5)
TO_LOG2 = SCALE * 1.4426950408889634
MIB = 1024 * 1024


def contract(left, right, left_dim, right_dim):
    return lax.dot_general(
        left, right, (((left_dim,), (right_dim,)), ((), ())), preferred_element_type=jnp.float32
    )


def tile_at(index):
    return pl.ds(pl.multiple_of(index * TILE, TILE), TILE)


def allowed_on_diagonal(key_group, row_group, row_dim):
    row = lax.broadcasted_iota(jnp.int32, (TILE, TILE), row_dim)
    column = lax.broadcasted_iota(jnp.int32, (TILE, TILE), 1 - row_dim)
    first_token = (row_group // HEAD_GROUPS) * QUERY_TOKENS
    row_place = (row // ROWS) * STRETCH + first_token + row % QUERY_TOKENS
    key_place = (column // KEY_TOKENS) * STRETCH + key_group * KEY_TOKENS + column % KEY_TOKENS
    return key_place <= row_place


def stats_kernel(table, scored, other_half, stats, query, key):
    key_group, row_group, core = table[PLACES], table[PLACES + 1], table[PLACES + 2]

    def prepare_rows(r):
        for s in range(SPAN):
            spot = slice(r * TILE + s * ROWS, r * TILE + (s + 1) * ROWS)
            scaled = scored[table[r * SPAN + s], 0:ROWS].astype(jnp.float32) * TO_LOG2
            high = scaled.astype(jnp.bfloat16)
            query[spot, 0:WIDTH] = high
            query[spot, WIDTH:] = (scaled - high.astype(jnp.float32)).astype(jnp.bfloat16)

    def prepare_keys(k):
        for s in range(SPAN):
            source = table[k * SPAN + s]
            start = k * TILE + s * KEY_TOKENS
            own_spot = pl.ds(pl.multiple_of(start + core * HALF, HALF), HALF)
            other_spot = pl.ds(pl.multiple_of(start + (1 - core) * HALF, HALF), HALF)
            own = scored[source, ROWS : ROWS + HALF]
            other = other_half[source, ROWS : ROWS + HALF]
            key[own_spot, 0:WIDTH] = own
            key[own_spot, WIDTH:] = own
            key[other_spot, 0:WIDTH] = other
            key[other_spot, WIDTH:] = other

    allowed = allowed_on_diagonal(key_group, row_group, 1)
    state = {}

    def absorb(r, first, masked):
        begin = HALF_TILE if masked and first % TILE >= HALF_TILE else 0
        rows = slice(r * TILE + begin, (r + 1) * TILE)
        scores = contract(key[first : first + CHUNK], query[rows], 1, 1)
        if masked:
            inside = first - r * TILE
            scores = jnp.where(allowed[inside : inside + CHUNK, begin:], scores, NEGATIVE)
        scores = scores.reshape(CHUNK // SUBLANES, SUBLANES, TILE - begin)
        for n in range(begin // HALF_TILE, 2):
            part = scores[..., n * HALF_TILE - begin : (n + 1) * HALF_TILE - begin]
            raised = jnp.max(part, axis=0)
            if (r, n) in state:
                highest, summed = state[r, n]
                raised = jnp.maximum(highest, raised)
                summed = summed * jnp.exp2(highest - raised)
                summed = summed + jnp.sum(jnp.exp2(part - raised[None]), axis=0)
            else:
                summed = jnp.sum(jnp.exp2(part - raised[None]), axis=0)
            state[r, n] = raised, summed

    def finish(r):
        for n in range(2):
            highest, summed = state.pop((r, n))
            row_peak = jnp.max(highest, axis=0, keepdims=True)
            row_total = jnp.sum(summed * jnp.exp2(highest - row_peak), axis=0, keepdims=True)
            lanes = slice(n * HALF_TILE, (n + 1) * HALF_TILE)
            stats[r : r + 1, lanes] = row_peak
            stats[r + TILES : r + TILES + 1, lanes] = row_total

    for first in range(0, ALL_KEYS, CHUNK):
        if first % TILE == 0:
            prepare_keys(first // TILE)
        for r in range(first // TILE, TILES):
            if first == 0:
                prepare_rows(r)
            absorb(r, first, r == first // TILE)
        if (first + CHUNK) % TILE == 0:
            finish(first // TILE)


def gradient_kernel(
    table,
    scored,
    swapped,
    weighed,
    stats_0,
    stats_1,
    stats_2,
    stats_3,
    own_grad,
    other_grad,
    query,
    grad,
    query_turned,
    grad_turned,
    key,
    value,
    logs,
    key_sorted,
    value_sorted,
    other_half,
    arrived,
):
    fetch = pltpu.make_async_copy(swapped.at[:, pl.ds(ROWS, 2 * HALF)], other_half, arrived)
    fetch.start()
    key_group, row_group, core = table[PLACES], table[PLACES + 1], table[PLACES + 2]
    lane = lax.broadcasted_iota(jnp.int32, (TILE, WIDTH), 1)
    row_token = lax.broadcasted_iota(jnp.int32, (ROWS, WIDTH), 0) % QUERY_TOKENS
    row_token = row_token + (row_group // HEAD_GROUPS) * QUERY_TOKENS
    own_lane = lax.broadcasted_iota(jnp.int32, (ROWS, WIDTH), 1) == row_token
    all_stats = [ref[...] for ref in (stats_0, stats_1, stats_2, stats_3)]
    peaks = [part[0:TILES] for part in all_stats]
    highest = jnp.maximum(jnp.maximum(peaks[0], peaks[1]), jnp.maximum(peaks[2], peaks[3]))
    summed = jnp.zeros_like(highest)
    for part in all_stats:
        summed = summed + part[TILES:] * jnp.exp2(part[0:TILES] - highest)
    log_totals = (highest + jnp.log2(summed)) * (1.0 / TO_LOG2)
    high = log_totals.astype(jnp.bfloat16).astype(jnp.float32)
    middle = (log_totals - high).astype(jnp.bfloat16).astype(jnp.float32)
    low = (log_totals - high - middle).astype(jnp.bfloat16).astype(jnp.float32)
    padding = jnp.zeros((WIDTH - 3 * TILES, TILE), jnp.float32)
    logs[...] = jnp.concatenate([high, middle, low, padding], axis=0).T
    allowed = allowed_on_diagonal(key_group, row_group, 0)
    key_extra = jnp.where(lane < 3 * TILES, -1.0, 0.0).astype(jnp.bfloat16)
    value_extra = jnp.full((TILE, WIDTH), -1.0, jnp.bfloat16)

    def tile_span(t):
        return slice(t * TILE, (t + 1) * TILE)

    def prepare_rows(r):
        here = tile_span(r)
        chosen = jnp.logical_and(lane % TILES == r, lane < 3 * TILES)
        query[here, WIDTH:] = jnp.where(chosen, logs[...], 0.0).astype(jnp.bfloat16)
        for k in range(SPAN):
            source = table[r * SPAN + k]
            spot = slice(r * TILE + k * ROWS, r * TILE + (k + 1) * ROWS)
            query[spot, 0:WIDTH] = scored[source, 0:ROWS]
            grad[spot, 0:WIDTH] = weighed[source, 0:ROWS]
            delta = weighed[source, ROWS : ROWS + SUBLANES].astype(jnp.float32)
            per_row = [
                jnp.broadcast_to(delta[h : h + 1], (QUERY_TOKENS, WIDTH)) for h in range(PAIR)
            ]
            grad[spot, WIDTH:] = jnp.where(own_lane, jnp.concatenate(per_row, axis=0), 0.0).astype(
                jnp.bfloat16
            )
        query_turned[:, here] = query[here, 0:WIDTH].T
        grad_turned[:, here] = grad[here, 0:WIDTH].T

    def prepare_keys(k):
        here = tile_span(k)
        key[here, WIDTH:] = key_extra
        value[here, WIDTH:] = value_extra
        for s in range(SPAN):
            source = table[k * SPAN + s]
            start = k * TILE + s * KEY_TOKENS
            own_spot = pl.ds(pl.multiple_of(start + core * HALF, HALF), HALF)
            other_spot = pl.ds(pl.multiple_of(start + (1 - core) * HALF, HALF), HALF)
            key[own_spot, 0:WIDTH] = scored[source, ROWS : ROWS + HALF]
            key[other_spot, 0:WIDTH] = other_half[source, 0:HALF]
            value[own_spot, 0:WIDTH] = scored[source, ROWS + HALF : ROWS + 2 * HALF]
            value[other_spot, 0:WIDTH] = other_half[source, HALF:]

    def first(rows_at, keys_at, masked):
        scores = contract(query[rows_at], key[keys_at], 1, 1)
        probs = jnp.exp2(scores * TO_LOG2)
        if masked:
            probs = jnp.where(allowed[: scores.shape[0], : scores.shape[1]], probs, 0.0)
        moved_probs = contract(grad[rows_at], value[keys_at], 1, 1)
        return probs.astype(jnp.bfloat16), (probs * moved_probs).astype(jnp.bfloat16)

    value_sums, key_sums, query_sums = {}, {}, {}

    def add(sums, spot, part):
        sums[spot] = sums[spot] + part if spot in sums else part

    def second(r, k, rows_at, keys_at, probs_low, dscores):
        value_part = contract(grad_turned[:, rows_at], probs_low, 1, 0)
        key_part = contract(query_turned[:, rows_at], dscores, 1, 0)
        query_part = contract(dscores, key[keys_at, 0:WIDTH], 1, 0)
        row_start = rows_at.start - r * TILE
        key_start = keys_at.start - k * TILE
        for n in range((rows_at.stop - rows_at.start) // HALF_TILE):
            span = slice(n * HALF_TILE, (n + 1) * HALF_TILE)
            add(query_sums, (r, row_start // HALF_TILE + n), query_part[span])
        for n in range((keys_at.stop - keys_at.start) // HALF_TILE):
            span = slice(n * HALF_TILE, (n + 1) * HALF_TILE)
            add(value_sums, (k, key_start // HALF_TILE + n), value_part[:, span])
            add(key_sums, (k, key_start // HALF_TILE + n), key_part[:, span])

    def finish_rows(r):
        for n in range(2):
            total = (query_sums.pop((r, n)) * SCALE).astype(jnp.bfloat16)
            for s in range(SPAN // 2):
                source = table[r * SPAN + n * SPAN // 2 + s]
                own_grad[source, 0:ROWS] = total[s * ROWS : (s + 1) * ROWS]

    def finish_keys(k):
        for n in range(2):
            here = slice(k * TILE + n * HALF_TILE, k * TILE + (n + 1) * HALF_TILE)
            key_sorted[here] = (key_sums.pop((k, n)) * SCALE).astype(jnp.bfloat16).T
            value_sorted[here] = value_sums.pop((k, n)).astype(jnp.bfloat16).T
            for s in range(n * SPAN // 2, (n + 1) * SPAN // 2):
                source = table[k * SPAN + s]
                start = k * TILE + s * KEY_TOKENS
                own_spot = pl.ds(pl.multiple_of(start + core * HALF, HALF), HALF)
                other_spot = pl.ds(pl.multiple_of(start + (1 - core) * HALF, HALF), HALF)
                own_grad[source, ROWS : ROWS + HALF] = key_sorted[own_spot]
                own_grad[source, ROWS + HALF :] = value_sorted[own_spot]
                other_grad[source, 0:HALF] = key_sorted[other_spot]
                other_grad[source, HALF:] = value_sorted[other_spot]

    def blocks():
        for k in range(TILES):
            middle = k * TILE + HALF_TILE
            late = slice(middle, (k + 1) * TILE)
            yield k, k, tile_span(k), slice(k * TILE, middle), True
            yield k, k, late, late, True
            for r in range(k + 1, TILES):
                yield r, k, tile_span(r), tile_span(k), False

    left = {}
    for r, k, *_ in blocks():
        left["rows", r] = left.get(("rows", r), 0) + 1
        left["keys", k] = left.get(("keys", k), 0) + 1

    def retire(r, k, *rest):
        second(r, k, *rest)
        left["rows", r] -= 1
        left["keys", k] -= 1
        if left["rows", r] == 0:
            finish_rows(r)
        if left["keys", k] == 0:
            finish_keys(k)

    waiting = []
    ready = {("rows", 0)}
    prepare_rows(0)
    fetch.wait()
    for r, k, rows_at, keys_at, masked in blocks():
        if k not in ready:
            ready.add(k)
            prepare_keys(k)
        if k == 0 and ("rows", r) not in ready:
            ready.add(("rows", r))
            prepare_rows(r)
        waiting.append((r, k, rows_at, keys_at) + first(rows_at, keys_at, masked))
        if len(waiting) > SKEW:
            retire(*waiting.pop(0))
    for entry in waiting:
        retire(*entry)


IN_VMEM = pl.BlockSpec(memory_space=pltpu.VMEM)
IN_SMEM = pl.BlockSpec(memory_space=pltpu.SMEM)
PAIRS = TILE * TILE * TILES * (TILES + 1) // 2


def stats_call(table, scored, other_half):
    return pl.pallas_call(
        stats_kernel,
        out_shape=jax.ShapeDtypeStruct((2 * TILES, TILE), jnp.float32),
        in_specs=[IN_SMEM, IN_VMEM, IN_VMEM],
        out_specs=IN_VMEM,
        scratch_shapes=[
            pltpu.VMEM((ALL_ROWS, 2 * WIDTH), jnp.bfloat16),
            pltpu.VMEM((ALL_KEYS, 2 * WIDTH), jnp.bfloat16),
        ],
        compiler_params=pltpu.CompilerParams(vmem_limit_bytes=20 * MIB),
        cost_estimate=pl.CostEstimate(
            flops=2 * PAIRS * WIDTH, bytes_accessed=4 * MIB, transcendentals=PAIRS
        ),
        name="softmax_totals",
    )(table, scored, other_half)


def gradient_call(table, scored, other_half, weighed, stats):
    own = jax.ShapeDtypeStruct((PLACES, ROWS + 2 * HALF, WIDTH), jnp.bfloat16)
    other = jax.ShapeDtypeStruct((PLACES, 2 * HALF, WIDTH), jnp.bfloat16)
    return pl.pallas_call(
        gradient_kernel,
        out_shape=(own, other),
        in_specs=[IN_SMEM, IN_VMEM, pl.BlockSpec(memory_space=pl.ANY)] + [IN_VMEM] * 5,
        out_specs=(IN_VMEM,) * 2,
        scratch_shapes=[
            pltpu.VMEM((ALL_ROWS, 2 * WIDTH), jnp.bfloat16),
            pltpu.VMEM((ALL_ROWS, 2 * WIDTH), jnp.bfloat16),
            pltpu.VMEM((WIDTH, ALL_ROWS), jnp.bfloat16),
            pltpu.VMEM((WIDTH, ALL_ROWS), jnp.bfloat16),
            pltpu.VMEM((ALL_KEYS, 2 * WIDTH), jnp.bfloat16),
            pltpu.VMEM((ALL_KEYS, 2 * WIDTH), jnp.bfloat16),
            pltpu.VMEM((TILE, WIDTH), jnp.float32),
            pltpu.VMEM((ALL_KEYS, WIDTH), jnp.bfloat16),
            pltpu.VMEM((ALL_KEYS, WIDTH), jnp.bfloat16),
            pltpu.VMEM((PLACES, 2 * HALF, WIDTH), jnp.bfloat16),
            pltpu.SemaphoreType.DMA,
        ],
        compiler_params=pltpu.CompilerParams(vmem_limit_bytes=32 * MIB),
        cost_estimate=pl.CostEstimate(
            flops=10 * PAIRS * WIDTH, bytes_accessed=8 * MIB, transcendentals=PAIRS
        ),
        name="gradients",
    )(table, scored, other_half, weighed, *stats)


def pack_rows(rows, outgoing):
    for r in range(ROW_GROUPS):
        tokens = (r // HEAD_GROUPS) * QUERY_TOKENS
        for h in range(PAIR):
            head = (r % HEAD_GROUPS) * PAIR + h
            part = rows[tokens : tokens + QUERY_TOKENS, head * WIDTH : (head + 1) * WIDTH]
            for g in range(KEY_GROUPS):
                outgoing[
                    g * ROW_GROUPS + r, h * QUERY_TOKENS : (h + 1) * QUERY_TOKENS
                ] = part


def pack_kernel(rows, keys, values, outgoing):
    pack_rows(rows, outgoing)
    for g in range(KEY_GROUPS):
        for c in range(2):
            first = g * KEY_TOKENS + c * HALF
            for n, array in enumerate((keys, values)):
                part = array[first : first + HALF]
                spot = slice(ROWS + n * HALF, ROWS + (n + 1) * HALF)
                for r in range(c, ROW_GROUPS, 2):
                    outgoing[g * ROW_GROUPS + r, spot] = part


def pack_grad_kernel(rows, forward, outgoing):
    pack_rows(rows, outgoing)
    lane = lax.broadcasted_iota(jnp.int32, (STRETCH, WIDTH), 1)
    delta = jnp.zeros((STRETCH, WIDTH), jnp.float32)
    for head in range(HEADS):
        span = slice(head * WIDTH, (head + 1) * WIDTH)
        products = rows[:, span].astype(jnp.float32) * forward[:, span].astype(jnp.float32)
        delta = jnp.where(lane == head, jnp.sum(products, axis=1, keepdims=True), delta)
    delta = delta.T
    blank = jnp.zeros((SUBLANES - PAIR, WIDTH), jnp.float32)
    for p in range(HEAD_GROUPS):
        part = jnp.concatenate([delta[PAIR * p : PAIR * (p + 1)], blank], axis=0)
        part = part.astype(jnp.bfloat16)
        for r in range(p, DEVICES, HEAD_GROUPS):
            outgoing[r, ROWS : ROWS + SUBLANES] = part


def pack_call(kernel, height, *arrays):
    return pl.pallas_call(
        kernel,
        out_shape=jax.ShapeDtypeStruct((DEVICES, height, WIDTH), jnp.bfloat16),
        in_specs=[IN_VMEM] * len(arrays),
        out_specs=IN_VMEM,
        compiler_params=pltpu.CompilerParams(vmem_limit_bytes=56 * MIB),
        name="pack",
    )(*arrays)


def pair_kernel(own, received, outgoing):
    outgoing[:, 0:ROWS] = own[:, 0:ROWS]
    total = own[:, ROWS:].astype(jnp.float32) + received[...].astype(jnp.float32)
    outgoing[:, ROWS:] = total.astype(jnp.bfloat16)


def pair_call(own, received):
    return pl.pallas_call(
        pair_kernel,
        out_shape=jax.ShapeDtypeStruct(own.shape, own.dtype),
        in_specs=[IN_VMEM] * 2,
        out_specs=IN_VMEM,
        compiler_params=pltpu.CompilerParams(vmem_limit_bytes=16 * MIB),
        name="pair_sum",
    )(own, received)


def sums_kernel(back, d_query, d_key, d_value):
    for r in range(ROW_GROUPS):
        total = back[r, 0:ROWS].astype(jnp.float32)
        for g in range(1, KEY_GROUPS):
            total = total + back[g * ROW_GROUPS + r, 0:ROWS].astype(jnp.float32)
        total = total.astype(jnp.bfloat16)
        tokens = (r // HEAD_GROUPS) * QUERY_TOKENS
        for h in range(PAIR):
            head = (r % HEAD_GROUPS) * PAIR + h
            d_query[tokens : tokens + QUERY_TOKENS, head * WIDTH : (head + 1) * WIDTH] = total[
                h * QUERY_TOKENS : (h + 1) * QUERY_TOKENS
            ]
    for g in range(KEY_GROUPS):
        for c in range(2):
            total = jnp.zeros((2 * HALF, WIDTH), jnp.float32)
            for r in range(c, ROW_GROUPS, 2):
                total = total + back[g * ROW_GROUPS + r, ROWS:].astype(jnp.float32)
            first = g * KEY_TOKENS + c * HALF
            d_key[first : first + HALF] = total[0:HALF].astype(jnp.bfloat16)
            d_value[first : first + HALF] = total[HALF:].astype(jnp.bfloat16)


def sums_call(back):
    small = jax.ShapeDtypeStruct((STRETCH, WIDTH), jnp.bfloat16)
    return pl.pallas_call(
        sums_kernel,
        out_shape=(
            jax.ShapeDtypeStruct((STRETCH, HEADS * WIDTH), jnp.bfloat16),
            small,
            small,
        ),
        in_specs=[IN_VMEM],
        out_specs=(IN_VMEM,) * 3,
        compiler_params=pltpu.CompilerParams(vmem_limit_bytes=12 * MIB),
        name="sums",
    )(back)


def shards(queries, key_states, value_states, out_grad, forward_out, stretch_order):
    me = lax.axis_index(ALL)
    swap = [(d, d ^ 1) for d in range(DEVICES)]

    def around(step):
        return [(d, (d + step * ROW_GROUPS) % DEVICES) for d in range(DEVICES)]

    with jax.named_scope("outgoing"):
        scored = pack_call(pack_kernel, ROWS + 2 * HALF, queries, key_states, value_states)
        weighed = pack_call(pack_grad_kernel, ROWS + SUBLANES, out_grad, forward_out)
    with jax.named_scope("table"):
        places = jnp.arange(PLACES, dtype=jnp.int32)
        holder = jnp.sum(
            jnp.where(stretch_order[None, :] == places[:, None], places[None, :], 0), axis=1
        )
        ids = jnp.stack([me // ROW_GROUPS, me % ROW_GROUPS, me % 2]).astype(jnp.int32)
        table = jnp.concatenate([holder, ids])
    with jax.named_scope("exchange_in"):
        scored = lax.all_to_all(scored, ALL, split_axis=0, concat_axis=0, tiled=True)
        scored, weighed = lax.optimization_barrier((scored, weighed))
        weighed = lax.all_to_all(weighed, ALL, split_axis=0, concat_axis=0, tiled=True)
        other_half = lax.ppermute(scored, ALL, swap)
    with jax.named_scope("totals"):
        stats = stats_call(table, scored, other_half)
        all_stats = [stats] + [lax.ppermute(stats, ALL, around(k)) for k in range(1, KEY_GROUPS)]
        weighed, all_stats = lax.optimization_barrier((weighed, all_stats))
    with jax.named_scope("gradients"):
        own_grad, other_grad = gradient_call(
            table, scored, other_half, weighed, all_stats
        )
    with jax.named_scope("exchange_out"):
        received = lax.ppermute(other_grad, ALL, swap)
        outgoing = pair_call(own_grad, received)
        back = lax.all_to_all(outgoing, ALL, split_axis=0, concat_axis=0, tiled=True)
    with jax.named_scope("sums"):
        return sums_call(back)


def solution(mesh):
    split = P(ALL, None)
    return jax.shard_map(
        shards,
        mesh=mesh,
        in_specs=(split,) * 5 + (P(),),
        out_specs=(split,) * 3,
        check_vma=False,
    )
```
